256 devices in a mesh: gx: 8 (over z), gy: 32 (over y, x, core).
Axes of the slice: x: 4, y: 4, z: 8, core: 2. Of those that a mesh axis runs over, the one named last changes fastest.
Arguments:
- design: float32 [128, 256, 1024], P('gx', 'gy'), may hold values from 0 to 1
- filtered: float32 [128, 256, 1024], P('gx', 'gy'), may hold values from 0 to 1
- sensitivity: float32 [128, 256, 1024], P('gx', 'gy'), may hold values from -400 to 400
- first_moment: float32 [128, 256, 1024], P('gx', 'gy'), may hold values from -0.6 to 0.6
- second_moment: float32 [128, 256, 1024], P('gx', 'gy'), may hold values from 0.001 to 0.1
- lagrange: float32 [2], replicated, may hold values from 0.5 to 2
- trace_values: float32 [8, 2048, 128], P('gx', 'gy'), may hold values from -6 to 6
- trace_anchor: int32 [8, 2048], P('gx', 'gy'), may hold values from 0 to 1023
- trace_owner: int32 [8, 2048, 1], P('gx', 'gy'), may hold values from 0 to 31; in each aligned block of 64 rows (0 to 63, 64 to 127, ..., all dimensions but the last counted through in order) at most 8 rows name the same one
Outputs:
- new_design: float32 [128, 256, 1024], P('gx', 'gy')
- new_first: float32 [128, 256, 1024], P('gx', 'gy')
- new_second: float32 [128, 256, 1024], P('gx', 'gy')
- gradient: float32 [128, 256, 1024], P('gx', 'gy')
The draws below stay inside these ranges and needn't reach their ends.
Inputs may be any that keep to these rules, and one draw needn't show every extreme that they name: `trace_owner`: among the 64 rows of one device no gy index is named more than 8 times; some index is named exactly 8 times.
All inputs are finite; a program needn't handle non-finite values.
Results may differ from the reference program's by a relative error of at most 0.00002.
Values sent between devices are 32-bit elements; how exact they have to be, the bound alone decides.
No kernel may reach another device: no remote copies, remote signals or barrier semaphores. Data moves between devices by JAX's collectives and lax.ppermute only.
A program may use at most 64 MiB of HBM per device.

```python
import math
import jax
import jax.numpy as jnp
import numpy as np

CX = 16
CY = 8
NZ = 1024
ROW = 128
BLK_DEV = 64
CAP = 8
SWEEPS = 4
ADAM_STEP = 10
NX = 128
NY = 256
N_GX = 8
N_GY = 32


def ramp_grid():
    first_pos = jnp.arange(NX, dtype=jnp.float32)[:, None, None] / (NX - 1)
    second_pos = jnp.arange(NY, dtype=jnp.float32)[None, :, None] / (NY - 1)
    return (first_pos, second_pos)


def draw_sensitivity(key, part):
    key = jax.random.fold_in(key, 11)
    base_key, rough_key = jax.random.split(key)
    first_pos, second_pos = ramp_grid()
    rising = jnp.exp(math.log(3.0) * (first_pos + second_pos))
    rough = jnp.exp(jax.random.uniform(rough_key, (NX, NY, NZ), jnp.float32, 0.0, math.log(10.0)))
    base = jnp.clip(jax.random.normal(base_key, (NX, NY, NZ), jnp.float32), -4.0, 4.0)
    return (base * rough * rising).astype(jnp.float32)


def draw_filtered(key, part):
    key = jax.random.fold_in(key, 23)
    first_pos, second_pos = ramp_grid()
    scale = (1.0 + (first_pos + second_pos)) / 3.0
    values = jax.random.uniform(key, (NX, NY, NZ), jnp.float32, 0.0, 1.0)
    return (values * scale).astype(jnp.float32)


def set_ends(result, rng, least, high):
    extent = result.shape
    index_at = [jax.random.randint(jax.random.fold_in(rng, axis), (), 0, extent[axis]) for axis in range(len(extent))]
    result = result.at[tuple(index_at)].set(least)
    longest = extent.index(max(extent))
    index_at[longest] = (index_at[longest] + 1) % extent[longest]
    return result.at[tuple(index_at)].set(high)


def steps_of(own_key, dims, cuts, smallest, largest):
    def one(position, blocks):
        steps = jax.random.uniform(jax.random.fold_in(jax.random.fold_in(own_key, 6), position), (blocks,), jnp.float32, smallest / len(cuts), largest / len(cuts))
        return jnp.repeat(jnp.exp(steps), dims[position] // blocks).reshape((-1,) + (1,) * (len(dims) - position - 1))

    factor_of = one(*cuts[0])
    for cut in cuts[1:]:
        factor_of = factor_of * one(*cut)
    return factor_of


def shared_out(stream_key, own, number, rows, number_of, top, bound, skew):
    sequence = jax.random.permutation(stream_key, number_of)
    heavy_load, ordinary = shares(number_of, rows * top, bound, skew, True), shares(number_of, rows * top, bound, skew, False)
    places = jnp.arange(number_of)

    def named(tallies, offset_by):
        used = int((tallies > 0).sum())
        fixed = max(1, used // 4)
        moved = fixed + (places - fixed + offset_by * (used - fixed)) % max(1, number_of - fixed)
        return jnp.zeros((number_of,), jnp.int32).at[sequence[jnp.where(places < fixed, places, moved)]].set(jnp.asarray(tallies, jnp.int32))

    tallies = jnp.where(number % 4 == 0, named(heavy_load, number // 4), named(ordinary, number - number // 4 - 1))
    mixed = jax.random.permutation(jax.random.fold_in(own, 3), number_of)
    giver, sink = mixed[0:number_of // 2 * 2:2], mixed[1:number_of // 2 * 2:2]
    margin = jnp.minimum(tallies[giver] - 1, bound - tallies[sink]) // 2
    margin = jnp.where((giver == sequence[0]) | (sink == sequence[0]) | (tallies[sink] == 0), 0, jnp.maximum(margin, 0))
    moved = jax.random.randint(jax.random.fold_in(own, 4), (number_of // 2,), 0, 1 << 20) % (margin + 1)
    tallies = tallies.at[giver].add(-moved).at[sink].add(moved)
    labels = jnp.searchsorted(jnp.cumsum(tallies), jnp.arange(rows * top), side="right").astype(jnp.int32)
    table = labels.reshape(top, rows).T
    table = table[jax.random.permutation(jax.random.fold_in(own, 1), rows)]
    offset_by = jax.random.randint(jax.random.fold_in(own, 2), (rows, 1), 0, top)
    return jnp.take_along_axis(table, (jnp.arange(top)[None, :] + offset_by) % top, axis=1)


def shares(count, total, most, skew, full):
    portions = [(1 << 20) // math.isqrt(grade ** skew) + 1 for grade in range(1, count + 1)]
    largest = most if full else min(most, max(-(-total // count), total * portions[0] // sum(portions)))
    least = 1 if total - largest >= count - 1 else 0
    given, surplus = [largest] + [least] * (count - 1), total - largest - least * (count - 1)
    while surplus > 0:
        movable = [i for i in range(1, count) if given[i] < largest] or [i for i in range(1, count) if given[i] < most]
        mass, budget = sum([portions[i] for i in movable]), surplus
        for i in movable:
            addition = min(most - given[i], max(1, budget * portions[i] // mass), surplus)
            given[i] = given[i] + addition
            surplus = surplus - addition
    return np.array(given)


def normal_values(own_key, extent, deviation, limit, cuts=(), held_as=jnp.bfloat16):
    values = deviation * jax.random.normal(own_key, extent, jnp.float32)
    if cuts:
        values = values * steps_of(own_key, extent, cuts, -0.22, 0.18)
    return jnp.clip(values, -limit, limit).astype(held_as)


def setup_inputs(seed: int = 0) -> dict:
    key_of = jax.random.split(jax.random.key(seed), 10)
    design = jnp.clip(1.0 * jax.random.uniform(key_of[0], (NX, NY, NZ), jnp.float32) ** steps_of(key_of[0], (NX, NY, NZ), ((0, 8), (1, 32)), -0.2, 0.2), 0.0, 1.0)
    filtered = draw_filtered(jax.random.fold_in(key_of[9], 71), 0)
    sensitivity = draw_sensitivity(jax.random.fold_in(key_of[9], 71), 0)
    first_moment = normal_values(key_of[3], (NX, NY, NZ), 0.1, 0.6, ((0, 8), (1, 32)), jnp.float32)
    second_moment = jnp.clip(jnp.exp(math.log(0.1) - 4.6051702 * jax.random.uniform(key_of[4], (NX, NY, NZ), jnp.float32) ** steps_of(key_of[4], (NX, NY, NZ), ((0, 8), (1, 32)), -0.2, 0.2)), 0.001, 0.1)
    lagrange = jnp.clip(jax.random.uniform(key_of[5], (2,), jnp.float32, 0.5, 2.0), 0.5, 2.0)
    trace_values = normal_values(key_of[6], (N_GX, N_GY * BLK_DEV, ROW), 1.0, 6.0, ((0, 8), (1, 32)), jnp.float32)
    trace_anchor = set_ends(jax.random.randint(key_of[7], (N_GX, N_GY * BLK_DEV), 0, CX * CY * NZ // ROW), jax.random.fold_in(key_of[7], 1), 0, (CX * CY * NZ // ROW) - 1).astype(jnp.int32)
    trace_owner_keys = jax.random.split(jax.random.fold_in(key_of[8], 1), N_GX * (N_GY * BLK_DEV) // BLK_DEV)
    trace_owner_turns = jax.random.permutation(jax.random.fold_in(key_of[8], 3), N_GX * (N_GY * BLK_DEV) // BLK_DEV)
    trace_owner = jax.vmap(lambda own, number: shared_out(jax.random.fold_in(key_of[8], 2), own, number, BLK_DEV, N_GY, 1, CAP, 2))(trace_owner_keys, trace_owner_turns).reshape((N_GX, N_GY * BLK_DEV, 1))
    return dict(design=design, filtered=filtered, sensitivity=sensitivity, first_moment=first_moment, second_moment=second_moment, lagrange=lagrange, trace_values=trace_values, trace_anchor=trace_anchor, trace_owner=trace_owner)


def smooth(source):
    field = source
    for sweep in range(SWEEPS):
        padded = jnp.pad(field, ((1, 1), (1, 1), (0, 0)))
        zpadded = jnp.pad(field, ((0, 0), (0, 0), (1, 1)))
        nearby = padded[2:, 1:-1] + padded[:-2, 1:-1] + padded[1:-1, 2:] + padded[1:-1, :-2]
        nearby = nearby + zpadded[:, :, 2:] + zpadded[:, :, :-2]
        field = (source + 4.0 * nearby) / 25.0
    return field

def reference(design, filtered, sensitivity, first_moment, second_moment, lagrange, trace_values, trace_anchor, trace_owner):
    slope_part = jnp.tanh(8.0 * (filtered - 0.5))
    denominator = 2.0 * jnp.tanh(4.0)
    projected = (jnp.tanh(4.0) + slope_part) / denominator
    slope = 8.0 * (1.0 - slope_part * slope_part) / denominator
    cells = NX * NY * NZ
    volume = jnp.sum(projected)
    weight = lagrange[0] + lagrange[1] * (volume / cells / 0.4 - 1.0)
    rows = jnp.zeros((N_GX, N_GY, CX * CY * NZ // ROW, ROW), jnp.float32)
    source_gx = jnp.broadcast_to(jnp.arange(N_GX, dtype=jnp.int32)[:, None], trace_anchor.shape)
    rows = rows.at[source_gx, trace_owner[:, :, 0], trace_anchor].add(trace_values)
    trace_field = rows.reshape(N_GX, N_GY, CX, CY, NZ).transpose(0, 2, 1, 3, 4).reshape(NX, NY, NZ)
    source = slope * (sensitivity + trace_field + weight)
    raw = smooth(source)
    gradient = raw / jnp.sqrt(jnp.sum(raw * raw) / cells + 1e-06)
    new_first = 0.9 * first_moment + 0.1 * gradient
    new_second = 0.999 * second_moment + 0.001 * gradient * gradient
    first_hat = new_first / (1.0 - 0.9 ** ADAM_STEP)
    second_hat = new_second / (1.0 - 0.999 ** ADAM_STEP)
    new_design = jnp.clip(design - 0.05 * first_hat / (jnp.sqrt(second_hat) + 1e-08), 0.0, 1.0)
    return (new_design, new_first, new_second, gradient)
```

```python
import functools

import jax
import jax.numpy as jnp
from jax import lax
from jax.experimental import pallas as pl
from jax.experimental.pallas import tpu as pltpu
from jax.sharding import PartitionSpec as P

SWEEPS = 4
ADAM_STEP = 10
CAP = 8
LANES = 128
HALO = 4
F32 = jnp.float32
HIGHEST = lax.Precision.HIGHEST
VMEM_LIMIT = 40 * 1024 * 1024


def params():
    return pltpu.CompilerParams(vmem_limit_bytes=VMEM_LIMIT)


def vmem():
    return pl.BlockSpec(memory_space=pltpu.VMEM)


def smem():
    return pl.BlockSpec(memory_space=pltpu.SMEM)


def iota(shape, dim):
    return lax.broadcasted_iota(jnp.int32, shape, dim)


def bucket_kernel(width_z, values_ref, anchor_ref, owner_ref, out_ref):
    rows = values_ref.shape[0]
    owners = out_ref.shape[0]
    owner = owner_ref[...]
    anchor = anchor_ref[...]
    chunks = width_z // LANES
    place = (anchor // (8 * chunks)) * (8 * chunks) + (anchor % chunks) * 8 + (anchor // chunks) % 8
    down = iota((rows, rows), 0)
    across = iota((rows, rows), 1)
    owner_f = owner.astype(F32)
    owner_column = jnp.sum(
        jnp.where(down == across, jnp.broadcast_to(owner_f, (rows, rows)), 0.0), axis=1, keepdims=True
    )
    earlier = (owner_column == owner_f) & (down < across)
    rank = jnp.sum(jnp.where(earlier, 1.0, 0.0), axis=0, keepdims=True)
    slot = iota((owners * CAP, rows), 0)
    chosen = (slot // CAP == owner) & ((slot % CAP).astype(F32) == rank)
    packed = jnp.dot(
        jnp.where(chosen, 1.0, 0.0), values_ref[...], precision=HIGHEST, preferred_element_type=F32
    )
    out_ref[:, 0:CAP, :] = packed.reshape(owners, CAP, LANES)
    named = jnp.where(iota((owners, rows), 0) == owner, 1.0, 0.0)
    lane = iota((LANES, rows), 0)
    marked = jnp.where((lane % CAP).astype(F32) == rank, place.astype(F32) + 1.0, 0.0)
    anchors = lax.dot_general(
        named, marked, (((1,), (1,)), ((), ())), precision=HIGHEST, preferred_element_type=F32
    )
    out_ref[:, CAP : 2 * CAP, :] = jnp.broadcast_to(anchors[:, None, :] - 1.0, (owners, CAP, LANES))


def bucket(values, anchor, owner, owners, width_z):
    return pl.pallas_call(
        functools.partial(bucket_kernel, width_z),
        out_shape=jax.ShapeDtypeStruct((owners, 2 * CAP, LANES), F32),
        in_specs=[vmem()] * 3,
        out_specs=vmem(),
        compiler_params=params(),
    )(values, anchor, owner)


def source_kernel(recv_ref, filtered_ref, sensitivity_ref, lagrange_ref, s_ref, low_ref, high_ref, volume_ref, field):
    width_x, width_y, width_z = filtered_ref.shape
    chunks = width_z // LANES
    owners = recv_ref.shape[0]
    group = LANES // CAP
    sent = recv_ref[:, CAP, :]
    peer = iota(sent.shape, 0)
    lane = iota(sent.shape, 1)
    kept = jnp.where(lane // CAP == peer % group, sent + 1.0, 0.0)
    anchors = [
        jnp.sum(kept[g : g + group], axis=0, keepdims=True) - 1.0 for g in range(0, owners, group)
    ]
    anchors = jnp.concatenate(anchors, axis=1) if len(anchors) > 1 else anchors[0][:, : owners * CAP]
    values = recv_ref[:, 0:CAP, :].reshape(owners * CAP, LANES)
    top = values.astype(jnp.bfloat16)
    rest = values - top.astype(F32)
    middle = rest.astype(jnp.bfloat16)
    last = (rest - middle.astype(F32)).astype(jnp.bfloat16)
    parts = jnp.concatenate([top, middle, last], axis=1)
    block_rows = width_x * width_y * chunks
    step = min(block_rows, 256)
    for start in range(0, block_rows, step):
        row = (iota((step, owners * CAP), 0) + start).astype(F32)
        hot = jnp.where(row == anchors, 1.0, 0.0).astype(jnp.bfloat16)
        added = jnp.dot(hot, parts, preferred_element_type=F32)
        field[start : start + step, :] = (
            added[:, 0:LANES] + added[:, LANES : 2 * LANES] + added[:, 2 * LANES : 3 * LANES]
        )
    base = lagrange_ref[0] + 0.25 * lagrange_ref[1]
    edge = jnp.tanh(jnp.full((8, LANES), 4.0, F32))
    inverse = 1.0 / (edge + edge)
    eight = 8.0 * inverse

    def layer(x, total):
        for c in range(chunks):
            at = pl.ds(c * LANES, LANES)
            part = jnp.tanh(8.0 * (filtered_ref[x, :, at] - 0.5))
            total = total + (edge + part) * inverse
            slope = (1.0 - part * part) * eight
            trace = field[pl.ds(pl.multiple_of((x * chunks + c) * 8, 8), 8), :]
            s_ref[0, x, :, at] = slope * ((sensitivity_ref[x, :, at] + trace) + base)
            s_ref[1, x, :, at] = slope
        return total

    volume_ref[...] = lax.fori_loop(0, width_x, layer, jnp.zeros((8, LANES), F32))
    low_ref[...] = s_ref[:, 0:HALO]
    high_ref[...] = s_ref[:, width_x - HALO :]


def make_source(recv, filtered, sensitivity, lagrange):
    width_x, width_y, width_z = filtered.shape
    face = jax.ShapeDtypeStruct((2, HALO, width_y, width_z), F32)
    return pl.pallas_call(
        source_kernel,
        out_shape=(
            jax.ShapeDtypeStruct((2, width_x, width_y, width_z), F32),
            face,
            face,
            jax.ShapeDtypeStruct((8, LANES), F32),
        ),
        in_specs=[vmem(), vmem(), vmem(), smem()],
        out_specs=(vmem(),) * 4,
        scratch_shapes=[pltpu.VMEM((width_x * width_y * width_z // LANES, LANES), F32)],
        compiler_params=params(),
    )(recv, filtered, sensitivity, lagrange)


def pack_kernel(s_ref, left_ref, right_ref, low_ref, high_ref):
    width_x, width_y, width_z = s_ref.shape[1:]
    row = iota((width_y, width_z), 0)
    half = row < 4
    for f in range(2):
        for i in range(width_x // 2):
            even, odd = s_ref[f, 2 * i], pltpu.roll(s_ref[f, 2 * i + 1], 4, 0)
            low_ref[f, i] = jnp.where(half, even, odd)
            high_ref[f, i] = jnp.where(half, odd, even)
        for i, (near, mid, far) in enumerate(
            ((left_ref[f, 3], left_ref[f, 2], left_ref[f, 1]), (right_ref[f, 0], right_ref[f, 1], right_ref[f, 2]))
        ):
            tile = width_x // 2 + i
            mid = pltpu.roll(mid, 4, 0)
            low_ref[f, tile] = jnp.where(row < 3, near, jnp.where(row == 3, pltpu.roll(far, 3, 0), mid))
            high_ref[f, tile] = jnp.where(row > 4, near, jnp.where(row == 4, pltpu.roll(far, 5, 0), mid))


def pack(s, left, right):
    _, width_x, width_y, width_z = s.shape
    face = jax.ShapeDtypeStruct((2, width_x // 2 + 2, width_y, width_z), F32)
    return pl.pallas_call(
        pack_kernel,
        out_shape=(face, face),
        in_specs=[vmem()] * 3,
        out_specs=(vmem(),) * 2,
        compiler_params=params(),
    )(s, left, right)


def smooth_kernel(
    s_ref, left_ref, right_ref, above_ref, below_ref, volume_ref, inside_ref, raw_ref, sums_ref, source, first, second
):
    width_x, width_y, width_z = s_ref.shape[1:]
    chunks = width_z // LANES
    layers = width_x + 2 * HALO
    inside_left = inside_ref[0]
    inside_right = inside_ref[1]
    row = iota((width_y, LANES), 0)
    lane = iota((width_y, LANES), 1)
    half = row < 4
    rim = jnp.where(half, inside_ref[3], inside_ref[2])
    wide_half = iota((width_y, width_z), 0) < 4
    wide_rim = jnp.where(wide_half, inside_ref[3], inside_ref[2])

    for f in range(2):
        source[f, 0, 0:HALO] = left_ref[f] * inside_left
        source[f, 0, HALO : HALO + width_x] = s_ref[f]
        source[f, 0, HALO + width_x :] = right_ref[f] * inside_right
        for i in range(width_x // 2):
            low, high = above_ref[f, i], below_ref[f, i]
            source[f, 1, HALO + 2 * i] = jnp.where(wide_half, low, high) * wide_rim
            source[f, 1, HALO + 2 * i + 1] = pltpu.roll(jnp.where(wide_half, high, low), 4, 0) * wide_rim
        for i, (near, step, keep) in enumerate(((HALO - 1, -1, inside_left), (HALO + width_x, 1, inside_right))):
            low, high = above_ref[f, width_x // 2 + i], below_ref[f, width_x // 2 + i]
            scale = wide_rim * keep
            source[f, 1, near] = jnp.where(wide_half, low, high) * scale
            source[f, 1, near + step] = pltpu.roll(jnp.where(wide_half, high, low), 4, 0) * scale
            source[f, 1, near + 2 * step] = (
                jnp.where(wide_half, pltpu.roll(low, 5, 0), pltpu.roll(high, 3, 0)) * scale
            )
            source[f, 1, near + 3 * step] = jnp.zeros((width_y, width_z), F32)

    def load(ref, f, tile, x):
        return [ref[f, tile, x, :, pl.ds(c * LANES, LANES)] for c in range(chunks)]

    def along_z(v):
        up = [pltpu.roll(t, LANES - 1, 1) for t in v]
        down = [pltpu.roll(t, 1, 1) for t in v]
        zero = jnp.zeros_like(v[0])
        return [
            jnp.where(lane == LANES - 1, up[c + 1] if c + 1 < chunks else zero, up[c])
            + jnp.where(lane == 0, down[c - 1] if c else zero, down[c])
            for c in range(chunks)
        ]

    def step(ref, f, x, both, weight):
        a, b = load(ref, f, 0, x), load(ref, f, 1, x)
        results = []
        a_z = along_z(a)
        b_z = along_z(b) if both else None
        out_a, out_b = [], []
        for c in range(chunks):
            at = pl.ds(c * LANES, LANES)
            a_up, b_up = pltpu.roll(a[c], 7, 0), pltpu.roll(b[c], 7, 0)
            a_down, b_down = pltpu.roll(a[c], 1, 0), pltpu.roll(b[c], 1, 0)
            sum_a = jnp.where(row == 7, b_up, a_up) + jnp.where(row == 0, b_down, a_down)
            sum_a = sum_a + a_z[c] + (ref[f, 0, x - 1, :, at] + ref[f, 0, x + 1, :, at])
            out_a.append(sum_a + weight * source[f, 0, x, :, at])
            if both:
                sum_b = jnp.where(row == 7, a_up, b_up) + jnp.where(row == 0, a_down, b_down)
                sum_b = sum_b + b_z[c] + (ref[f, 1, x - 1, :, at] + ref[f, 1, x + 1, :, at])
                out_b.append((sum_b + weight * source[f, 1, x, :, at]) * rim)
        return out_a, out_b

    def store(ref, f, tile, x, values, keep=None):
        for c in range(chunks):
            ref[f, tile, x, :, pl.ds(c * LANES, LANES)] = values[c] if keep is None else values[c] * keep

    refs = (source, first, second, first)
    for k in range(1, SWEEPS):
        weight = (25.0 / 4.0) ** k / 25.0
        reach = SWEEPS - k
        old, new = refs[k - 1], refs[k]
        for f in range(2):

            def body(x, carry, f=f, old=old, new=new, weight=weight):
                a, b = step(old, f, x, True, weight)
                store(new, f, 0, x, a)
                store(new, f, 1, x, b)
                return carry

            lax.fori_loop(HALO, HALO + width_x, body, 0)
            for d in range(1, reach + 1):
                for x, keep in ((HALO - d, inside_left), (HALO + width_x - 1 + d, inside_right)):
                    a, b = step(old, f, x, d < reach, weight)
                    store(new, f, 0, x, a, keep)
                    if b:
                        store(new, f, 1, x, b, keep)

    last = refs[SWEEPS - 1]
    weight = (25.0 / 4.0) ** SWEEPS / 25.0
    scale = (4.0 / 25.0) ** SWEEPS

    def finish(x, sums):
        one, _ = step(last, 0, x + HALO, False, weight)
        two, _ = step(last, 1, x + HALO, False, weight)
        aa, ab, bb = sums
        for c in range(chunks):
            at = pl.ds(c * LANES, LANES)
            u, v = one[c] * scale, two[c] * scale
            raw_ref[0, x, :, at] = u
            raw_ref[1, x, :, at] = v
            aa, ab, bb = aa + u * u, ab + u * v, bb + v * v
        return aa, ab, bb

    zeros = jnp.zeros((8, LANES), F32)
    aa, ab, bb = lax.fori_loop(0, width_x, finish, (zeros, zeros, zeros))
    rows = [jnp.sum(t, axis=0, keepdims=True) for t in (volume_ref[...], aa, ab, bb)]
    tile = jnp.where(
        row == 0, rows[0], jnp.where(row == 1, rows[1], jnp.where(row == 2, rows[2], jnp.where(row == 3, rows[3], 0.0)))
    )
    for i in range(sums_ref.shape[0]):
        sums_ref[i] = tile


def smooth(s, left, right, above, below, volume, inside, copies):
    _, width_x, width_y, width_z = s.shape
    extended = pltpu.VMEM((2, 2, width_x + 2 * HALO, width_y, width_z), F32)
    return pl.pallas_call(
        smooth_kernel,
        out_shape=(
            jax.ShapeDtypeStruct(s.shape, F32),
            jax.ShapeDtypeStruct((copies, 8, LANES), F32),
        ),
        in_specs=[vmem()] * 6 + [smem()],
        out_specs=(vmem(),) * 2,
        scratch_shapes=[extended] * 3,
        compiler_params=params(),
    )(s, left, right, above, below, volume, inside)


def adam_kernel(
    cells, sums_ref, lagrange_ref, raw_ref, design_ref, first_ref, second_ref, d_ref, m_ref, v_ref, g_ref
):
    sums = jnp.sum(sums_ref[...], axis=0)
    volume = jnp.sum(sums[0:1], axis=1, keepdims=True)
    shift = lagrange_ref[1] * (volume / cells / 0.4 - 1.25)
    total = jnp.sum(sums[1:2] + 2.0 * shift * sums[2:3] + shift * shift * sums[3:4], axis=1, keepdims=True)
    inverse = 1.0 / jnp.sqrt(jnp.maximum(total, 0.0) / cells + 1e-06)
    gradient = (raw_ref[0] + shift[:, :, None] * raw_ref[1]) * inverse[:, :, None]
    new_first = 0.9 * first_ref[...] + 0.1 * gradient
    new_second = 0.999 * second_ref[...] + 0.001 * gradient * gradient
    first_hat = new_first / (1.0 - 0.9**ADAM_STEP)
    second_hat = new_second / (1.0 - 0.999**ADAM_STEP)
    d_ref[...] = jnp.clip(design_ref[...] - 0.05 * first_hat / (jnp.sqrt(second_hat) + 1e-08), 0.0, 1.0)
    m_ref[...] = new_first
    v_ref[...] = new_second
    g_ref[...] = gradient


def adam(cells, sums, lagrange, raw, design, first_moment, second_moment):
    width_x, width_y, width_z = design.shape
    steps = 4
    block = (width_x // steps, width_y, width_z)
    spec = pl.BlockSpec(block, lambda i: (i, 0, 0))
    return pl.pallas_call(
        functools.partial(adam_kernel, cells),
        grid=(steps,),
        out_shape=(jax.ShapeDtypeStruct(design.shape, F32),) * 4,
        in_specs=[
            pl.BlockSpec(sums.shape, lambda i: (0, 0, 0)),
            smem(),
            pl.BlockSpec((2,) + block, lambda i: (0, i, 0, 0)),
            spec,
            spec,
            spec,
        ],
        out_specs=(spec,) * 4,
        compiler_params=params(),
    )(sums, lagrange, raw, design, first_moment, second_moment)


def shift(cells, axis, by):
    count = lax.axis_size(axis)
    return lax.ppermute(cells, axis, [(i, (i + by) % count) for i in range(count)])


def per_device(
    design,
    filtered,
    sensitivity,
    first_moment,
    second_moment,
    lagrange,
    trace_values,
    trace_anchor,
    trace_owner,
):
    width_x, width_y, depth = design.shape
    count_x, count_y = lax.axis_size("gx"), lax.axis_size("gy")
    cells = float(width_x * width_y * depth * count_x * count_y)
    index_x, index_y = lax.axis_index("gx"), lax.axis_index("gy")
    inside = jnp.stack([index_x > 0, index_x < count_x - 1, index_y > 0, index_y < count_y - 1]).astype(F32)

    rows = trace_values.shape[1]
    sent = bucket(trace_values[0], trace_anchor, trace_owner.reshape(1, rows), count_y, depth)
    received = lax.all_to_all(sent, "gy", 0, 0, tiled=True)
    s, low, high, volume = make_source(received, filtered, sensitivity, lagrange)
    left, right = shift(high, "gx", 1), shift(low, "gx", -1)
    low, high = pack(s, left, right)
    below, above = shift(high, "gy", 1), shift(low, "gy", -1)
    raw, sums = smooth(s, left, right, above, below, volume, inside, count_x)
    sums = jnp.sum(lax.all_to_all(sums, "gx", 0, 0, tiled=True), axis=0)
    sums = lax.all_to_all(jnp.broadcast_to(sums[None], (count_y,) + sums.shape), "gy", 0, 0, tiled=True)
    return adam(cells, sums, lagrange, raw, design, first_moment, second_moment)


def solution(mesh):
    block = P("gx", "gy", None)
    return jax.shard_map(
        per_device,
        mesh=mesh,
        in_specs=(block, block, block, block, block, P(), block, P("gx", "gy"), block),
        out_specs=(block, block, block, block),
        check_vma=False,
    )
```

```python
import functools

import jax
import jax.numpy as jnp
from jax import lax
from jax.experimental import pallas as pl
from jax.experimental.pallas import tpu as pltpu
from jax.sharding import PartitionSpec as P

SWEEPS = 4
ADAM_STEP = 10
CAP = 8
LANES = 128
HALO = 4
TALL = 16
GUARD = 8
FACE_ROWS = (8, 10, 12, 14)
FACE = sum(FACE_ROWS)
F32 = jnp.float32
BF16 = jnp.bfloat16
HIGHEST = lax.Precision.HIGHEST
MIB = 1024 * 1024


def params(mib):
    return pltpu.CompilerParams(vmem_limit_bytes=mib * MIB)


VMEM = pl.BlockSpec(memory_space=pltpu.VMEM)
SMEM = pl.BlockSpec(memory_space=pltpu.SMEM)
HBM = pl.BlockSpec(memory_space=pltpu.HBM)


def iota(shape, dim):
    return lax.broadcasted_iota(jnp.int32, shape, dim)


def start_all(pairs, sems):
    copies = [pltpu.make_async_copy(src, dst, sems.at[i]) for i, (src, dst) in enumerate(pairs)]
    for copy in copies:
        copy.start()
    return copies


def send_kernel(
    values_hbm, anchor_hbm, owner_hbm, filtered_hbm, sensitivity_hbm,
    out_ref, low_ref, high_ref, filtered_ref, sensitivity_ref,
    values_ref, anchor_ref, owner_ref, sems,
):
    copies = start_all(
        (
            (anchor_hbm, anchor_ref),
            (owner_hbm, owner_ref),
            (values_hbm, values_ref),
            (filtered_hbm, filtered_ref),
            (sensitivity_hbm, sensitivity_ref),
        ),
        sems,
    )
    width_x, width_y, width_z = filtered_ref.shape
    chunks = width_z // LANES
    rows = values_ref.shape[0]
    owners = out_ref.shape[0]
    copies[0].wait()
    copies[1].wait()
    owner = owner_ref[...]
    anchor = anchor_ref[...]
    place = (anchor // (8 * chunks)) * (8 * chunks) + (anchor % chunks) * 8 + (anchor // chunks) % 8
    down = iota((rows, rows), 0)
    across = iota((rows, rows), 1)
    owner_f = owner.astype(F32)
    owner_column = jnp.sum(
        jnp.where(down == across, jnp.broadcast_to(owner_f, (rows, rows)), 0.0), axis=1, keepdims=True
    )
    earlier = (owner_column == owner_f) & (down < across)
    rank = jnp.sum(jnp.where(earlier, 1.0, 0.0), axis=0, keepdims=True)
    slot = iota((owners * CAP, rows), 0)
    chosen = jnp.where((slot // CAP == owner) & ((slot % CAP).astype(F32) == rank), 1.0, 0.0)
    named = jnp.where(iota((owners, rows), 0) == owner, 1.0, 0.0)
    lane = iota((LANES, rows), 0)
    marked = jnp.where((lane % CAP).astype(F32) == rank, place.astype(F32) + 1.0, 0.0)
    anchors = lax.dot_general(
        named, marked, (((1,), (1,)), ((), ())), precision=HIGHEST, preferred_element_type=F32
    )
    lower = (anchors.astype(jnp.int32) - 1) % 8 < 4
    blank = jnp.zeros((1, LANES), F32)
    from_next = jnp.concatenate([jnp.where(lower, anchors, 0.0)[1:], blank], axis=0)
    from_last = jnp.concatenate([blank, jnp.where(lower, 0.0, anchors)[:-1]], axis=0)
    for i, line in enumerate((anchors, from_next, from_last)):
        out_ref[:, 3 * CAP + i, :] = line
    copies[2].wait()
    packed = jnp.dot(chosen, values_ref[...], precision=HIGHEST, preferred_element_type=F32)
    packed = packed.reshape(owners, CAP, LANES)
    nothing = jnp.zeros((1, CAP, LANES), F32)
    out_ref[:, 0:CAP, :] = packed
    out_ref[0 : owners - 1, CAP : 2 * CAP, :] = packed[1:]
    out_ref[owners - 1 :, CAP : 2 * CAP, :] = nothing
    out_ref[1:, 2 * CAP : 3 * CAP, :] = packed[:-1]
    out_ref[0:1, 2 * CAP : 3 * CAP, :] = nothing
    half = iota((width_y, width_z), 0) < 4
    for f, ref in enumerate((filtered_ref, sensitivity_ref)):
        copies[3 + f].wait()
        for i in range(width_x // 2):
            even, odd = ref[2 * i], pltpu.roll(ref[2 * i + 1], 4, 0)
            low_ref[f, i] = jnp.where(half, even, odd)
            high_ref[f, i] = jnp.where(half, odd, even)


def make_send(values, anchor, owner, filtered, sensitivity, owners):
    width_x, width_y, width_z = filtered.shape
    block = jax.ShapeDtypeStruct(filtered.shape, F32)
    face = jax.ShapeDtypeStruct((2, width_x // 2, width_y, width_z), F32)
    return pl.pallas_call(
        send_kernel,
        out_shape=(jax.ShapeDtypeStruct((owners, 4 * CAP, LANES), F32), face, face, block, block),
        in_specs=[HBM] * 5,
        out_specs=(VMEM,) * 5,
        scratch_shapes=[
            pltpu.VMEM(values.shape, F32),
            pltpu.VMEM(anchor.shape, jnp.int32),
            pltpu.VMEM(owner.shape, jnp.int32),
            pltpu.SemaphoreType.DMA((5,)),
        ],
        compiler_params=params(4),
    )(values, anchor, owner, filtered, sensitivity)


def exact_parts(values):
    top = values.astype(BF16)
    rest = values - top.astype(F32)
    middle = rest.astype(BF16)
    last = (rest - middle.astype(F32)).astype(BF16)
    return jnp.concatenate([top, middle, last], axis=1)


def source_kernel(
    recv_ref, filtered_ref, sensitivity_ref, above_ref, below_ref, lagrange_ref, inside_ref,
    s_ref, low_ref, high_ref, volume_ref, own, beside,
):
    width_x, width_y, width_z = filtered_ref.shape
    chunks = width_z // LANES
    owners = recv_ref.shape[0]
    group = min(LANES // CAP, owners)
    peer = iota((owners, LANES), 0)
    lane = iota((owners, LANES), 1)

    def places(line):
        kept = jnp.where(lane // CAP == peer % group, recv_ref[:, line, :], 0.0)
        sums = [jnp.sum(kept[g : g + group], axis=0, keepdims=True) for g in range(0, owners, group)]
        return [t[:, : group * CAP] for t in sums]

    def slots(start):
        return recv_ref[:, start : start + CAP, :].reshape(owners * CAP, LANES)

    block_rows = width_x * width_y * chunks
    step = min(block_rows, 256)
    for ref, lines, starts in ((own, (24,), (0,)), (beside, (25, 26), (8, 16))):
        anchors = jnp.concatenate([p for line in lines for p in places(line)], axis=1)
        parts = jnp.concatenate([exact_parts(slots(start)) for start in starts], axis=0)
        for start in range(0, block_rows, step):
            row = (iota((step, anchors.shape[1]), 0) + (start + 1)).astype(F32)
            hot = jnp.where(row == anchors, 1.0, 0.0).astype(BF16)
            added = jnp.dot(hot, parts, preferred_element_type=F32)
            ref[start : start + step, :] = (
                added[:, 0:LANES] + added[:, LANES : 2 * LANES] + added[:, 2 * LANES : 3 * LANES]
            )
    base = lagrange_ref[0] + 0.25 * lagrange_ref[1]
    edge = jnp.tanh(jnp.full((8, LANES), 4.0, F32))
    inverse = 1.0 / (edge + edge)
    eight = 8.0 * inverse
    half = iota((width_y, LANES), 0) < 4
    rim = jnp.where(half, inside_ref[3], inside_ref[2]) * eight

    def pair(i, total):
        for c in range(chunks):
            at = pl.ds(c * LANES, LANES)
            sides = [(above_ref[f, i, :, at], below_ref[f, i, :, at]) for f in range(2)]
            for odd in range(2):
                x = 2 * i + odd
                line = pl.ds(pl.multiple_of((x * chunks + c) * 8, 8), 8)
                part = jnp.tanh(8.0 * (filtered_ref[x, :, at] - 0.5))
                total = total + (edge + part) * inverse
                slope = (1.0 - part * part) * eight
                source = slope * ((sensitivity_ref[x, :, at] + own[line, :]) + base)
                density, sense = [
                    pltpu.roll(jnp.where(half, high, low), 4, 0) if odd else jnp.where(half, low, high)
                    for low, high in sides
                ]
                part = jnp.tanh(8.0 * (density - 0.5))
                slope_out = (1.0 - part * part) * rim
                source_out = slope_out * ((sense + beside[line, :]) + base)
                row = pl.multiple_of((x * chunks + c) * TALL, TALL)
                for f, (inner, outer) in enumerate(((source, source_out), (slope, slope_out))):
                    s_ref[f, pl.ds(row, 8), :] = pltpu.roll(jnp.where(half, inner, outer), 4, 0)
                    s_ref[f, pl.ds(row + 8, 8), :] = pltpu.roll(jnp.where(half, outer, inner), 4, 0)
        return total

    volume_ref[...] = lax.fori_loop(0, width_x // 2, pair, jnp.zeros((8, LANES), F32))
    for f in range(2):
        for c in range(chunks):
            to = f * FACE
            for d, count in zip(range(HALO, 0, -1), FACE_ROWS):
                skip = (TALL - count) // 2
                for ref, x in ((low_ref, d - 1), (high_ref, width_x - d)):
                    row = (x * chunks + c) * TALL + skip
                    ref[c, to : to + count, :] = s_ref[f, row : row + count, :]
                to += count


def make_source(recv, filtered, sensitivity, above, below, lagrange, inside):
    width_x, width_y, width_z = filtered.shape
    chunks = width_z // LANES
    face = jax.ShapeDtypeStruct((chunks, 2 * FACE, LANES), F32)
    scratch = pltpu.VMEM((width_x * width_y * chunks, LANES), F32)
    return pl.pallas_call(
        source_kernel,
        out_shape=(
            jax.ShapeDtypeStruct((2, width_x * chunks * TALL, LANES), F32),
            face,
            face,
            jax.ShapeDtypeStruct((8, LANES), F32),
        ),
        in_specs=[VMEM] * 5 + [SMEM] * 2,
        out_specs=(VMEM,) * 4,
        scratch_shapes=[scratch] * 2,
        compiler_params=params(8),
    )(recv, filtered, sensitivity, above, below, lagrange, inside)


def smooth_kernel(
    s_ref, left_ref, right_ref, volume_ref, inside_ref, design_hbm, first_hbm, second_hbm,
    raw_ref, sums_ref, design_ref, first_ref, second_ref, source, one, two, sems,
):
    copies = start_all(((design_hbm, design_ref), (first_hbm, first_ref), (second_hbm, second_ref)), sems)
    width_x, width_y, width_z = raw_ref.shape[1:]
    chunks = width_z // LANES
    layer = chunks * TALL
    inside_left = inside_ref[0]
    inside_right = inside_ref[1]
    row = iota((width_y, LANES), 0)
    lane = iota((width_y, LANES), 1)
    half = row < 4
    rims = (jnp.where(half, inside_ref[2], 1.0), jnp.where(half, 1.0, inside_ref[3]))

    start = GUARD + HALO * layer
    for f in range(2):
        source[f, start : start + width_x * layer, :] = s_ref[f]
        for c in range(chunks):
            to = f * FACE
            for d, count in zip(range(HALO, 0, -1), FACE_ROWS):
                skip = (TALL - count) // 2
                for ref, x, keep in (
                    (left_ref, HALO - d, inside_left),
                    (right_ref, HALO + width_x - 1 + d, inside_right),
                ):
                    at = GUARD + x * layer + c * TALL + skip
                    source[f, at : at + count, :] = ref[c, to : to + count, :] * keep
                to += count

    def step(ref, f, base, weight):
        own = [ref[f, pl.ds(base + c * TALL, 8), :] for c in range(chunks)]
        up = [pltpu.roll(t, LANES - 1, 1) for t in own]
        down = [pltpu.roll(t, 1, 1) for t in own]
        zero = jnp.zeros((8, LANES), F32)
        results = []
        for c in range(chunks):
            at = base + c * TALL
            total = jnp.where(lane == LANES - 1, up[c + 1] if c + 1 < chunks else zero, up[c])
            total = total + jnp.where(lane == 0, down[c - 1] if c else zero, down[c])
            total = total + (ref[f, pl.ds(at - 1, 8), :] + ref[f, pl.ds(at + 1, 8), :])
            total = total + (ref[f, pl.ds(at - layer, 8), :] + ref[f, pl.ds(at + layer, 8), :])
            results.append(total + weight * source[f, pl.ds(at, 8), :])
        return results

    refs = (source, one, two, one)
    for k in range(1, SWEEPS):
        weight = (25.0 / 4.0) ** k / 25.0
        reach = SWEEPS - k
        old, new = refs[k - 1], refs[k]

        def body(x, carry, old=old, new=new, weight=weight):
            keep = jnp.where(x < HALO, inside_left, jnp.where(x >= HALO + width_x, inside_right, 1.0))
            for tile in range(2):
                mask = rims[tile] * keep
                base = pl.multiple_of(GUARD + x * layer + tile * 8, 8)
                for f in range(2):
                    for c, value in enumerate(step(old, f, base, weight)):
                        new[f, pl.ds(base + c * TALL, 8), :] = value * mask
            return carry

        lax.fori_loop(HALO - reach, HALO + width_x + reach, body, 0)

    weight = (25.0 / 4.0) ** SWEEPS / 25.0
    scale = (4.0 / 25.0) ** SWEEPS

    def finish(x, sums):
        base = GUARD + (x + HALO) * layer + HALO
        a, b = [step(refs[SWEEPS - 1], f, base, weight) for f in range(2)]
        aa, ab, bb = sums
        for c in range(chunks):
            at = pl.ds(c * LANES, LANES)
            u, v = a[c] * scale, b[c] * scale
            raw_ref[0, x, :, at] = u
            raw_ref[1, x, :, at] = v
            aa, ab, bb = aa + u * u, ab + u * v, bb + v * v
        return aa, ab, bb

    zeros = jnp.zeros((8, LANES), F32)
    aa, ab, bb = lax.fori_loop(0, width_x, finish, (zeros, zeros, zeros))
    rows = [jnp.sum(t, axis=0, keepdims=True) for t in (volume_ref[...], aa, ab, bb)]
    tile = jnp.where(
        row == 0, rows[0], jnp.where(row == 1, rows[1], jnp.where(row == 2, rows[2], jnp.where(row == 3, rows[3], 0.0)))
    )
    for i in range(sums_ref.shape[0]):
        sums_ref[i] = tile
    for copy in copies:
        copy.wait()


def smooth(s, left, right, volume, inside, design, first_moment, second_moment, copies):
    width_x, width_y, width_z = design.shape
    block = jax.ShapeDtypeStruct(design.shape, F32)
    extended = pltpu.VMEM((2, (width_x + 2 * HALO) * (width_z // LANES) * TALL + 2 * GUARD, LANES), F32)
    return pl.pallas_call(
        smooth_kernel,
        out_shape=(
            jax.ShapeDtypeStruct((2,) + design.shape, F32),
            jax.ShapeDtypeStruct((copies, 8, LANES), F32),
            block,
            block,
            block,
        ),
        in_specs=[VMEM] * 4 + [SMEM] + [HBM] * 3,
        out_specs=(VMEM,) * 5,
        scratch_shapes=[extended] * 3 + [pltpu.SemaphoreType.DMA((3,))],
        compiler_params=params(14),
    )(s, left, right, volume, inside, design, first_moment, second_moment)


def adam_kernel(
    cells, sums_ref, lagrange_ref, raw_ref, design_ref, first_ref, second_ref,
    d_hbm, m_hbm, v_hbm, g_hbm, d_ref, m_ref, v_ref, g_ref, sems,
):
    width_x = design_ref.shape[0]
    sums = jnp.sum(sums_ref[...], axis=0)
    volume = jnp.sum(sums[0:1], axis=1, keepdims=True)
    shift = lagrange_ref[1] * (volume / cells / 0.4 - 1.25)
    total = jnp.sum(sums[1:2] + 2.0 * shift * sums[2:3] + shift * shift * sums[3:4], axis=1, keepdims=True)
    inverse = 1.0 / jnp.sqrt(jnp.maximum(total, 0.0) / cells + 1e-06)
    blocks = 4
    size = width_x // blocks
    copies = []
    for block in range(blocks):
        part = pl.ds(block * size, size)

        def body(i, carry, block=block):
            x = block * size + i
            gradient = (raw_ref[0, x] + shift * raw_ref[1, x]) * inverse
            new_first = 0.9 * first_ref[x] + 0.1 * gradient
            new_second = 0.999 * second_ref[x] + 0.001 * gradient * gradient
            first_hat = new_first * (0.05 / (1.0 - 0.9**ADAM_STEP))
            second_hat = new_second * (1.0 / (1.0 - 0.999**ADAM_STEP))
            d_ref[x] = jnp.clip(design_ref[x] - first_hat / (jnp.sqrt(second_hat) + 1e-08), 0.0, 1.0)
            m_ref[x] = new_first
            v_ref[x] = new_second
            g_ref[x] = gradient
            return carry

        lax.fori_loop(0, size, body, 0)
        for i, (ref, hbm) in enumerate(((d_ref, d_hbm), (m_ref, m_hbm), (v_ref, v_hbm), (g_ref, g_hbm))):
            copy = pltpu.make_async_copy(ref.at[part], hbm.at[part], sems.at[block, i])
            copy.start()
            copies.append(copy)
    for copy in copies:
        copy.wait()


def adam(cells, sums, lagrange, raw, design, first_moment, second_moment):
    return pl.pallas_call(
        functools.partial(adam_kernel, cells),
        out_shape=(jax.ShapeDtypeStruct(design.shape, F32),) * 4,
        in_specs=[VMEM, SMEM] + [VMEM] * 4,
        out_specs=(HBM,) * 4,
        scratch_shapes=[pltpu.VMEM(design.shape, F32)] * 4 + [pltpu.SemaphoreType.DMA((4, 4))],
        compiler_params=params(6),
    )(sums, lagrange, raw, design, first_moment, second_moment)


def shift(cells, axis, by):
    count = lax.axis_size(axis)
    return lax.ppermute(cells, axis, [(i, (i + by) % count) for i in range(count)])


def per_device(
    design,
    filtered,
    sensitivity,
    first_moment,
    second_moment,
    lagrange,
    trace_values,
    trace_anchor,
    trace_owner,
):
    width_x, width_y, depth = design.shape
    count_x, count_y = lax.axis_size("gx"), lax.axis_size("gy")
    cells = float(width_x * width_y * depth * count_x * count_y)
    index_x, index_y = lax.axis_index("gx"), lax.axis_index("gy")
    inside = jnp.stack([index_x > 0, index_x < count_x - 1, index_y > 0, index_y < count_y - 1]).astype(F32)

    rows = trace_values.shape[1]
    sent, low, high, filtered, sensitivity = make_send(
        trace_values[0], trace_anchor, trace_owner.reshape(1, rows), filtered, sensitivity, count_y
    )
    below, above = shift(high, "gy", 1), shift(low, "gy", -1)
    received = lax.all_to_all(sent, "gy", 0, 0, tiled=True)
    s, low, high, volume = make_source(received, filtered, sensitivity, above, below, lagrange, inside)
    left, right = shift(high, "gx", 1), shift(low, "gx", -1)
    raw, sums, design, first_moment, second_moment = smooth(
        s, left, right, volume, inside, design, first_moment, second_moment, count_x
    )
    sums = jnp.sum(lax.all_to_all(sums, "gx", 0, 0, tiled=True), axis=0)
    sums = lax.all_to_all(jnp.broadcast_to(sums[None], (count_y,) + sums.shape), "gy", 0, 0, tiled=True)
    return adam(cells, sums, lagrange, raw, design, first_moment, second_moment)


def solution(mesh):
    block = P("gx", "gy", None)
    return jax.shard_map(
        per_device,
        mesh=mesh,
        in_specs=(block, block, block, block, block, P(), block, P("gx", "gy"), block),
        out_specs=(block, block, block, block),
        check_vma=False,
    )
```

```python
import functools

import jax
import jax.numpy as jnp
from jax import lax
from jax.experimental import pallas as pl
from jax.experimental.pallas import tpu as pltpu
from jax.sharding import PartitionSpec as P

SWEEPS = 4
ADAM_STEP = 10
CAP = 8
LANES = 128
HALO = 4
TALL = 16
GUARD = 8
FACE_ROWS = (8, 10, 12, 14)
FACE = sum(FACE_ROWS)
F32 = jnp.float32
BF16 = jnp.bfloat16
HIGHEST = lax.Precision.HIGHEST
MIB = 1024 * 1024


def params(mib):
    return pltpu.CompilerParams(vmem_limit_bytes=mib * MIB)


VMEM = pl.BlockSpec(memory_space=pltpu.VMEM)
SMEM = pl.BlockSpec(memory_space=pltpu.SMEM)
HBM = pl.BlockSpec(memory_space=pltpu.HBM)


def iota(shape, dim):
    return lax.broadcasted_iota(jnp.int32, shape, dim)


def in_hbm(array):
    return pltpu.with_memory_space_constraint(array, pltpu.HBM)


def start_all(pairs, sems):
    copies = [pltpu.make_async_copy(src, dst, sems.at[i]) for i, (src, dst) in enumerate(pairs)]
    for copy in copies:
        copy.start()
    return copies


def bucket_kernel(chunks, values_hbm, anchor_hbm, owner_hbm, out_ref, values_ref, anchor_ref, owner_ref, sems):
    copies = start_all(((anchor_hbm, anchor_ref), (owner_hbm, owner_ref), (values_hbm, values_ref)), sems)
    rows = values_ref.shape[0]
    owners = out_ref.shape[0]
    copies[0].wait()
    copies[1].wait()
    owner = owner_ref[...]
    anchor = anchor_ref[...]
    place = (anchor // (8 * chunks)) * (8 * chunks) + (anchor % chunks) * 8 + (anchor // chunks) % 8
    down = iota((rows, rows), 0)
    across = iota((rows, rows), 1)
    owner_f = owner.astype(F32)
    owner_column = jnp.sum(
        jnp.where(down == across, jnp.broadcast_to(owner_f, (rows, rows)), 0.0), axis=1, keepdims=True
    )
    earlier = (owner_column == owner_f) & (down < across)
    rank = jnp.sum(jnp.where(earlier, 1.0, 0.0), axis=0, keepdims=True)
    slot = iota((owners * CAP, rows), 0)
    chosen = jnp.where((slot // CAP == owner) & ((slot % CAP).astype(F32) == rank), 1.0, 0.0)
    named = jnp.where(iota((owners, rows), 0) == owner, 1.0, 0.0)
    lane = iota((LANES, rows), 0)
    marked = jnp.where((lane % CAP).astype(F32) == rank, place.astype(F32) + 1.0, 0.0)
    anchors = lax.dot_general(
        named, marked, (((1,), (1,)), ((), ())), precision=HIGHEST, preferred_element_type=F32
    )
    lower = (anchors.astype(jnp.int32) - 1) % 8 < 4
    blank = jnp.zeros((1, LANES), F32)
    from_next = jnp.concatenate([jnp.where(lower, anchors, 0.0)[1:], blank], axis=0)
    from_last = jnp.concatenate([blank, jnp.where(lower, 0.0, anchors)[:-1]], axis=0)
    for i, line in enumerate((anchors, from_next, from_last)):
        out_ref[:, 3 * CAP + i, :] = line
    copies[2].wait()
    packed = jnp.dot(chosen, values_ref[...], precision=HIGHEST, preferred_element_type=F32)
    packed = packed.reshape(owners, CAP, LANES)
    nothing = jnp.zeros((1, CAP, LANES), F32)
    out_ref[:, 0:CAP, :] = packed
    out_ref[0 : owners - 1, CAP : 2 * CAP, :] = packed[1:]
    out_ref[owners - 1 :, CAP : 2 * CAP, :] = nothing
    out_ref[1:, 2 * CAP : 3 * CAP, :] = packed[:-1]
    out_ref[0:1, 2 * CAP : 3 * CAP, :] = nothing


def bucket(values, anchor, owner, owners, chunks):
    return pl.pallas_call(
        functools.partial(bucket_kernel, chunks),
        out_shape=jax.ShapeDtypeStruct((owners, 4 * CAP, LANES), F32),
        in_specs=[HBM] * 3,
        out_specs=VMEM,
        scratch_shapes=[
            pltpu.VMEM(values.shape, F32),
            pltpu.VMEM(anchor.shape, jnp.int32),
            pltpu.VMEM(owner.shape, jnp.int32),
            pltpu.SemaphoreType.DMA((3,)),
        ],
        compiler_params=params(4),
    )(in_hbm(values), in_hbm(anchor), in_hbm(owner))


def faces_kernel(filtered_hbm, sensitivity_hbm, low_ref, high_ref, filtered_ref, sensitivity_ref, sems):
    copies = start_all(((filtered_hbm, filtered_ref), (sensitivity_hbm, sensitivity_ref)), sems)
    width_x, width_y, width_z = filtered_ref.shape
    half = iota((width_y, width_z), 0) < 4
    for f, ref in enumerate((filtered_ref, sensitivity_ref)):
        copies[f].wait()
        for i in range(width_x // 2):
            even, odd = ref[2 * i], pltpu.roll(ref[2 * i + 1], 4, 0)
            low_ref[f, i] = jnp.where(half, even, odd)
            high_ref[f, i] = jnp.where(half, odd, even)


def make_faces(filtered, sensitivity):
    width_x, width_y, width_z = filtered.shape
    block = jax.ShapeDtypeStruct(filtered.shape, F32)
    face = jax.ShapeDtypeStruct((2, width_x // 2, width_y, width_z), F32)
    return pl.pallas_call(
        faces_kernel,
        out_shape=(face, face, block, block),
        in_specs=[HBM] * 2,
        out_specs=(VMEM,) * 4,
        scratch_shapes=[pltpu.SemaphoreType.DMA((2,))],
        compiler_params=params(4),
    )(in_hbm(filtered), in_hbm(sensitivity))


def exact_parts(values):
    top = values.astype(BF16)
    rest = values - top.astype(F32)
    middle = rest.astype(BF16)
    last = (rest - middle.astype(F32)).astype(BF16)
    return jnp.concatenate([top, middle, last], axis=1)


def scatter(recv_ref, own, beside, layers, layer_rows):
    owners = recv_ref.shape[0]
    group = min(LANES // CAP, owners)
    peer = iota((owners, LANES), 0)
    lane = iota((owners, LANES), 1)

    def places(line):
        kept = jnp.where(lane // CAP == peer % group, recv_ref[:, line, :], 0.0)
        sums = [jnp.sum(kept[g : g + group], axis=0, keepdims=True) for g in range(0, owners, group)]
        return [t[:, : group * CAP] for t in sums]

    def slots(start):
        return recv_ref[:, start : start + CAP, :].reshape(owners * CAP, LANES)

    for ref, lines, starts in ((own, (24,), (0,)), (beside, (25, 26), (8, 16))):
        anchors = jnp.concatenate([p for line in lines for p in places(line)], axis=1)
        parts = jnp.concatenate([exact_parts(slots(start)) for start in starts], axis=0)
        for first in layers:
            start, step = first * layer_rows, HALO * layer_rows
            row = (iota((step, anchors.shape[1]), 0) + (start + 1)).astype(F32)
            hot = jnp.where(row == anchors, 1.0, 0.0).astype(BF16)
            added = jnp.dot(hot, parts, preferred_element_type=F32)
            ref[start : start + step, :] = (
                added[:, 0:LANES] + added[:, LANES : 2 * LANES] + added[:, 2 * LANES : 3 * LANES]
            )


def source_pair(
    i, total, s_ref, filtered_ref, sensitivity_ref, above_ref, below_ref, own, beside, lagrange_ref, inside_ref
):
    width_x, width_y, width_z = filtered_ref.shape
    chunks = width_z // LANES
    base = lagrange_ref[0] + 0.25 * lagrange_ref[1]
    edge = jnp.tanh(jnp.full((8, LANES), 4.0, F32))
    inverse = 1.0 / (edge + edge)
    eight = 8.0 * inverse
    half = iota((width_y, LANES), 0) < 4
    rim = jnp.where(half, inside_ref[3], inside_ref[2]) * eight
    for c in range(chunks):
        at = pl.ds(c * LANES, LANES)
        sides = [(above_ref[f, i, :, at], below_ref[f, i, :, at]) for f in range(2)]
        for odd in range(2):
            x = 2 * i + odd
            line = pl.ds(pl.multiple_of((x * chunks + c) * 8, 8), 8)
            part = jnp.tanh(8.0 * (filtered_ref[x, :, at] - 0.5))
            total = total + (edge + part) * inverse
            slope = (1.0 - part * part) * eight
            source = slope * ((sensitivity_ref[x, :, at] + own[line, :]) + base)
            density, sense = [
                pltpu.roll(jnp.where(half, high, low), 4, 0) if odd else jnp.where(half, low, high)
                for low, high in sides
            ]
            part = jnp.tanh(8.0 * (density - 0.5))
            slope_out = (1.0 - part * part) * rim
            source_out = slope_out * ((sense + beside[line, :]) + base)
            row = pl.multiple_of(GUARD + ((x + HALO) * chunks + c) * TALL, 8)
            for f, (inner, outer) in enumerate(((source, source_out), (slope, slope_out))):
                s_ref[f, pl.ds(row, 8), :] = pltpu.roll(jnp.where(half, inner, outer), 4, 0)
                s_ref[f, pl.ds(row + 8, 8), :] = pltpu.roll(jnp.where(half, outer, inner), 4, 0)
    return total


def face_rows(chunks):
    for f in range(2):
        to = f * FACE
        for d, count in zip(range(HALO, 0, -1), FACE_ROWS):
            skip = (TALL - count) // 2
            for c in range(chunks):
                for more in sorted({0, count - 8}):
                    yield f, c, d, to + more, skip + more
            to += count


def edge_kernel(
    recv_ref, filtered_ref, sensitivity_ref, above_ref, below_ref, lagrange_ref, inside_ref,
    s_ref, low_ref, high_ref, volume_ref, own, beside,
):
    width_x, width_y, width_z = filtered_ref.shape
    chunks = width_z // LANES
    scatter(recv_ref, own, beside, (0, width_x - HALO), width_y * chunks)

    def pair(j, total):
        i = jnp.where(j < HALO // 2, j, j + (width_x - 2 * HALO) // 2)
        return source_pair(
            i, total, s_ref, filtered_ref, sensitivity_ref, above_ref, below_ref, own, beside, lagrange_ref, inside_ref
        )

    volume_ref[...] = lax.fori_loop(0, HALO, pair, jnp.zeros((8, LANES), F32))
    for f, c, d, to, skip in face_rows(chunks):
        for ref, x in ((low_ref, d - 1), (high_ref, width_x - d)):
            row = GUARD + ((x + HALO) * chunks + c) * TALL + skip
            ref[c, to : to + 8, :] = s_ref[f, row : row + 8, :]


def extended(shape):
    width_x, width_y, width_z = shape
    return jax.ShapeDtypeStruct((2, (width_x + 2 * HALO) * (width_z // LANES) * TALL + 2 * GUARD, LANES), F32)


def make_edges(recv, filtered, sensitivity, above, below, lagrange, inside):
    width_x, width_y, width_z = filtered.shape
    chunks = width_z // LANES
    face = jax.ShapeDtypeStruct((chunks, 2 * FACE, LANES), F32)
    scratch = pltpu.VMEM((width_x * width_y * chunks, LANES), F32)
    return pl.pallas_call(
        edge_kernel,
        out_shape=(extended(filtered.shape), face, face, jax.ShapeDtypeStruct((8, LANES), F32)),
        in_specs=[VMEM] * 5 + [SMEM] * 2,
        out_specs=(VMEM,) * 4,
        scratch_shapes=[scratch] * 2,
        compiler_params=params(8),
    )(recv, filtered, sensitivity, above, below, lagrange, inside)


def sweep(ref, source, f, base, weight, chunks):
    layer = chunks * TALL
    lane = iota((8, LANES), 1)
    own = [ref[f, pl.ds(base + c * TALL, 8), :] for c in range(chunks)]
    up = [pltpu.roll(t, LANES - 1, 1) for t in own]
    down = [pltpu.roll(t, 1, 1) for t in own]
    zero = jnp.zeros((8, LANES), F32)
    results = []
    for c in range(chunks):
        at = base + c * TALL
        total = jnp.where(lane == LANES - 1, up[c + 1] if c + 1 < chunks else zero, up[c])
        total = total + jnp.where(lane == 0, down[c - 1] if c else zero, down[c])
        total = total + (ref[f, pl.ds(at - 1, 8), :] + ref[f, pl.ds(at + 1, 8), :])
        total = total + (ref[f, pl.ds(at - layer, 8), :] + ref[f, pl.ds(at + layer, 8), :])
        results.append(total + weight * source[f, pl.ds(at, 8), :])
    return results


def sweep_layer(old, new, source, x, weight, rims, keep, chunks):
    layer = chunks * TALL
    for tile in range(2):
        mask = rims[tile] if keep is None else rims[tile] * keep
        base = pl.multiple_of(GUARD + x * layer + tile * 8, 8)
        for f in range(2):
            for c, value in enumerate(sweep(old, source, f, base, weight, chunks)):
                new[f, pl.ds(base + c * TALL, 8), :] = value * mask


def last_layer(old, source, raw_ref, x, sums, chunks):
    scale = (4.0 / 25.0) ** SWEEPS
    base = GUARD + (x + HALO) * chunks * TALL + HALO
    a, b = [sweep(old, source, f, base, weight_of(SWEEPS), chunks) for f in range(2)]
    aa, ab, bb = sums
    for c in range(chunks):
        at = pl.ds(c * LANES, LANES)
        u, v = a[c] * scale, b[c] * scale
        raw_ref[0, x, :, at] = u
        raw_ref[1, x, :, at] = v
        aa, ab, bb = aa + u * u, ab + u * v, bb + v * v
    return aa, ab, bb


def weight_of(k):
    return (25.0 / 4.0) ** k / 25.0


def rims_of(inside_ref):
    half = iota((8, LANES), 0) < 4
    return (jnp.where(half, inside_ref[2], 1.0), jnp.where(half, 1.0, inside_ref[3]))


def inner_kernel(
    recv_ref, filtered_ref, sensitivity_ref, above_ref, below_ref, lagrange_ref, inside_ref, volume_ref,
    design_hbm, first_hbm, second_hbm, edges_ref,
    s_ref, one, two, three, raw_ref, sums_ref, design_ref, first_ref, second_ref, own, beside, sems,
):
    del edges_ref
    copies = start_all(((design_hbm, design_ref), (first_hbm, first_ref), (second_hbm, second_ref)), sems)
    width_x, width_y, width_z = filtered_ref.shape
    chunks = width_z // LANES
    scatter(recv_ref, own, beside, range(HALO, width_x - HALO, HALO), width_y * chunks)

    def pair(i, total):
        return source_pair(
            i, total, s_ref, filtered_ref, sensitivity_ref, above_ref, below_ref, own, beside, lagrange_ref, inside_ref
        )

    sums_ref[0] = lax.fori_loop(HALO // 2, (width_x - HALO) // 2, pair, volume_ref[...])
    rims = rims_of(inside_ref)
    refs = (s_ref, one, two, three)
    for k in range(1, SWEEPS):

        def body(x, carry, k=k):
            sweep_layer(refs[k - 1], refs[k], s_ref, x + HALO, weight_of(k), rims, None, chunks)
            return carry

        lax.fori_loop(k, width_x - k, body, 0, unroll=2)
    zeros = jnp.zeros((8, LANES), F32)
    sums = lax.fori_loop(
        HALO,
        width_x - HALO,
        lambda x, sums: last_layer(three, s_ref, raw_ref, x, sums, chunks),
        (zeros, zeros, zeros),
        unroll=4,
    )
    for i in range(3):
        sums_ref[1 + i] = sums[i]
    for copy in copies:
        copy.wait()


def make_inner(
    recv, filtered, sensitivity, above, below, lagrange, inside, volume, design, first_moment, second_moment, edges
):
    width_x, width_y, width_z = filtered.shape
    block = jax.ShapeDtypeStruct(filtered.shape, F32)
    wide = extended(filtered.shape)
    scratch = pltpu.VMEM((width_x * width_y * width_z // LANES, LANES), F32)
    return pl.pallas_call(
        inner_kernel,
        out_shape=(
            wide,
            wide,
            wide,
            wide,
            jax.ShapeDtypeStruct((2,) + filtered.shape, F32),
            jax.ShapeDtypeStruct((4, 8, LANES), F32),
            block,
            block,
            block,
        ),
        in_specs=[VMEM] * 5 + [SMEM] * 2 + [VMEM] + [HBM] * 3 + [VMEM],
        out_specs=(VMEM,) * 9,
        input_output_aliases={11: 0},
        scratch_shapes=[scratch] * 2 + [pltpu.SemaphoreType.DMA((3,))],
        compiler_params=params(8),
        cost_estimate=pl.CostEstimate(flops=40_000_000, bytes_accessed=16_000_000, transcendentals=300_000),
    )(
        recv, filtered, sensitivity, above, below, lagrange, inside, volume,
        in_hbm(design), in_hbm(first_moment), in_hbm(second_moment), edges,
    )


def outer_kernel(
    left_ref, right_ref, inside_ref, sums_ref, s_in, one_in, two_in, three_in, raw_in,
    s_ref, one, two, three, raw_ref, send_ref,
):
    del s_in, one_in, two_in, three_in, raw_in
    width_x, width_y, width_z = raw_ref.shape[1:]
    chunks = width_z // LANES
    layer = chunks * TALL
    left, right = inside_ref[0], inside_ref[1]
    for f, c, d, to, skip in face_rows(chunks):
        for ref, x, keep in ((left_ref, HALO - d, left), (right_ref, HALO + width_x - 1 + d, right)):
            row = GUARD + x * layer + c * TALL + skip
            s_ref[f, row : row + 8, :] = ref[c, to : to + 8, :] * keep
    rims = rims_of(inside_ref)
    refs = (s_ref, one, two, three)
    for k in range(1, SWEEPS):

        def body(j, carry, k=k):
            x = j + k
            sweep_layer(
                refs[k - 1], refs[k], s_ref, x, weight_of(k), rims, jnp.where(x < HALO, left, 1.0), chunks
            )
            x = 2 * HALO + width_x - 1 - x
            sweep_layer(
                refs[k - 1], refs[k], s_ref, x, weight_of(k), rims, jnp.where(x >= HALO + width_x, right, 1.0), chunks
            )
            return carry

        lax.fori_loop(0, HALO, body, 0, unroll=2)

    def finish(x, sums):
        sums = last_layer(three, s_ref, raw_ref, x, sums, chunks)
        return last_layer(three, s_ref, raw_ref, width_x - 1 - x, sums, chunks)

    sums = lax.fori_loop(0, HALO, finish, tuple(sums_ref[1 + i] for i in range(3)), unroll=2)
    lane = iota((1, LANES), 1)
    line = jnp.zeros((1, LANES), F32)
    for i, tile in enumerate((sums_ref[0],) + tuple(sums)):
        total = jnp.sum(tile, axis=0, keepdims=True)
        total = total + pltpu.roll(total, LANES // 2, 1)
        total = total + pltpu.roll(total, LANES // 4, 1)
        line = jnp.where(lane // (LANES // 4) == i, total, line)
    send_ref[...] = jnp.broadcast_to(line, send_ref.shape)


def make_outer(left, right, inside, sums, wide, raw, copies):
    return pl.pallas_call(
        outer_kernel,
        out_shape=tuple(jax.ShapeDtypeStruct(w.shape, F32) for w in wide)
        + (
            jax.ShapeDtypeStruct(raw.shape, F32),
            jax.ShapeDtypeStruct((copies, LANES), F32),
        ),
        in_specs=[VMEM] * 2 + [SMEM] + [VMEM] * 6,
        out_specs=(VMEM,) * 6,
        input_output_aliases={4: 0, 5: 1, 6: 2, 7: 3, 8: 4},
        compiler_params=params(4),
    )(left, right, inside, sums, *wide, raw)[4:]


def adam_kernel(
    cells, sums_ref, lagrange_ref, raw_ref, design_ref, first_ref, second_ref,
    d_hbm, m_hbm, v_hbm, g_hbm, d_ref, m_ref, v_ref, g_ref, sems,
):
    width_x = design_ref.shape[0]
    line = jnp.sum(sums_ref[...], axis=0, keepdims=True)
    part = iota(line.shape, 1) // (LANES // 4)

    def picked(scale):
        return jnp.sum(line * scale, axis=1, keepdims=True)

    volume = picked(jnp.where(part == 0, 1.0, 0.0))
    shift = lagrange_ref[1] * (volume / cells / 0.4 - 1.25)
    total = picked(
        jnp.where(part == 1, 1.0, jnp.where(part == 2, 2.0 * shift, jnp.where(part == 3, shift * shift, 0.0)))
    )
    inverse = 1.0 / jnp.sqrt(jnp.maximum(total, 0.0) / cells + 1e-06)
    blocks = 4
    size = width_x // blocks
    copies = []
    for block in range(blocks):
        part = pl.ds(block * size, size)

        def body(i, carry, block=block):
            x = block * size + i
            gradient = (raw_ref[0, x] + shift * raw_ref[1, x]) * inverse
            new_first = 0.9 * first_ref[x] + 0.1 * gradient
            new_second = 0.999 * second_ref[x] + 0.001 * gradient * gradient
            first_hat = new_first * (0.05 / (1.0 - 0.9**ADAM_STEP))
            second_hat = new_second * (1.0 / (1.0 - 0.999**ADAM_STEP))
            d_ref[x] = jnp.clip(design_ref[x] - first_hat / (jnp.sqrt(second_hat) + 1e-08), 0.0, 1.0)
            m_ref[x] = new_first
            v_ref[x] = new_second
            g_ref[x] = gradient
            return carry

        lax.fori_loop(0, size, body, 0)
        for i, (ref, hbm) in enumerate(((d_ref, d_hbm), (m_ref, m_hbm), (v_ref, v_hbm), (g_ref, g_hbm))):
            copy = pltpu.make_async_copy(ref.at[part], hbm.at[part], sems.at[block, i])
            copy.start()
            copies.append(copy)
    for copy in copies:
        copy.wait()


def adam(cells, sums, lagrange, raw, design, first_moment, second_moment):
    return pl.pallas_call(
        functools.partial(adam_kernel, cells),
        out_shape=(jax.ShapeDtypeStruct(design.shape, F32),) * 4,
        in_specs=[VMEM, SMEM] + [VMEM] * 4,
        out_specs=(HBM,) * 4,
        scratch_shapes=[pltpu.VMEM(design.shape, F32)] * 4 + [pltpu.SemaphoreType.DMA((4, 4))],
        compiler_params=params(6),
    )(sums, lagrange, raw, design, first_moment, second_moment)


def shift(cells, axis, by):
    count = lax.axis_size(axis)
    return lax.ppermute(cells, axis, [(i, (i + by) % count) for i in range(count)])


def per_device(
    design,
    filtered,
    sensitivity,
    first_moment,
    second_moment,
    lagrange,
    trace_values,
    trace_anchor,
    trace_owner,
):
    width_x, width_y, depth = design.shape
    count_x, count_y = lax.axis_size("gx"), lax.axis_size("gy")
    cells = float(width_x * width_y * depth * count_x * count_y)
    index_x, index_y = lax.axis_index("gx"), lax.axis_index("gy")
    inside = jnp.stack([index_x > 0, index_x < count_x - 1, index_y > 0, index_y < count_y - 1]).astype(F32)

    rows = trace_values.shape[1]
    sent = bucket(trace_values[0], trace_anchor, trace_owner.reshape(1, rows), count_y, depth // LANES)
    received = lax.all_to_all(sent, "gy", 0, 0, tiled=True)
    low, high, filtered, sensitivity = make_faces(filtered, sensitivity)
    below, above = shift(high, "gy", 1), shift(low, "gy", -1)
    s, low, high, volume = make_edges(received, filtered, sensitivity, above, below, lagrange, inside)
    left, right = shift(high, "gx", 1), shift(low, "gx", -1)
    s, one, two, three, raw, sums, design, first_moment, second_moment = make_inner(
        received, filtered, sensitivity, above, below, lagrange, inside, volume,
        design, first_moment, second_moment, s,
    )
    raw, sums = make_outer(left, right, inside, sums, (s, one, two, three), raw, count_x * count_y)
    sums = lax.all_to_all(sums, ("gx", "gy"), 0, 0, tiled=True)
    return adam(cells, sums, lagrange, raw, design, first_moment, second_moment)


def solution(mesh):
    block = P("gx", "gy", None)
    return jax.shard_map(
        per_device,
        mesh=mesh,
        in_specs=(block, block, block, block, block, P(), block, P("gx", "gy"), block),
        out_specs=(block, block, block, block),
        check_vma=False,
    )
```

```python
import functools
import itertools

import jax
import jax.numpy as jnp
from jax import lax
from jax.experimental import pallas as pl
from jax.experimental.pallas import tpu as pltpu
from jax.sharding import PartitionSpec as P

SWEEPS = 4
ADAM_STEP = 10
CAP = 8
LANES = 128
HALO = 4
TALL = 16
GUARD = 8
FACE_ROWS = (8, 10, 12, 14)
FACE = sum(FACE_ROWS)
LEFT, RIGHT, RIM, RIM_HALO, BASE, PENALTY = 0, 1, 2, 4, 5, 6
F32 = jnp.float32
BF16 = jnp.bfloat16
HIGHEST = lax.Precision.HIGHEST
MIB = 1024 * 1024


def params(mib):
    return pltpu.CompilerParams(vmem_limit_bytes=mib * MIB)


VMEM = pl.BlockSpec(memory_space=pltpu.VMEM)
HBM = pl.BlockSpec(memory_space=pltpu.HBM)


def iota(shape, dim):
    return lax.broadcasted_iota(jnp.int32, shape, dim)


def in_hbm(array):
    return pltpu.with_memory_space_constraint(array, pltpu.HBM)


def start_all(pairs, sems):
    copies = [pltpu.make_async_copy(src, dst, sems.at[i]) for i, (src, dst) in enumerate(pairs)]
    for copy in copies:
        copy.start()
    return copies


def first_kernel(
    values_hbm, anchor_hbm, owner_hbm, lagrange_hbm, filtered_hbm, sensitivity_hbm,
    low_ref, high_ref, masks_ref, values_ref, anchor_ref, owner_ref, lagrange_ref, filtered_ref, sensitivity_ref, sems,
):
    copies = start_all(
        (
            (filtered_hbm, filtered_ref),
            (sensitivity_hbm, sensitivity_ref),
            (lagrange_hbm, lagrange_ref),
            (anchor_hbm, anchor_ref),
            (owner_hbm, owner_ref),
            (values_hbm, values_ref),
        ),
        sems,
    )
    width_x, width_y, width_z = filtered_ref.shape
    index_x, index_y = lax.axis_index("gx"), lax.axis_index("gy")
    one, zero = jnp.ones((8, LANES), F32), jnp.zeros((8, LANES), F32)
    upper = iota((8, LANES), 0) < 4
    before, after = jnp.where(index_y > 0, one, zero), jnp.where(index_y < lax.axis_size("gy") - 1, one, zero)
    masks_ref[LEFT] = jnp.where(index_x > 0, one, zero)
    masks_ref[RIGHT] = jnp.where(index_x < lax.axis_size("gx") - 1, one, zero)
    masks_ref[RIM] = jnp.where(upper, before, one)
    masks_ref[RIM + 1] = jnp.where(upper, one, after)
    masks_ref[RIM_HALO] = jnp.where(upper, after, before)
    half = iota((width_y, width_z), 0) < 4
    for f, ref in enumerate((filtered_ref, sensitivity_ref)):
        copies[f].wait()
        for i in range(width_x // 2):
            even, odd = ref[2 * i], pltpu.roll(ref[2 * i + 1], 4, 0)
            low_ref[f, i] = jnp.where(half, even, odd)
            high_ref[f, i] = jnp.where(half, odd, even)
    copies[2].wait()
    weight, penalty = lagrange_ref[0:1, 0:1], lagrange_ref[0:1, 1:2]
    masks_ref[BASE] = one * (weight + 0.25 * penalty)
    masks_ref[PENALTY] = one * penalty
    for copy in copies[3:]:
        copy.wait()


def make_first(values, anchor, owner, lagrange, filtered, sensitivity):
    width_x, width_y, width_z = filtered.shape
    face = jax.ShapeDtypeStruct((2, width_x // 2, width_y, width_z), F32)
    return pl.pallas_call(
        first_kernel,
        out_shape=(
            face,
            face,
            jax.ShapeDtypeStruct((7, 8, LANES), F32),
            jax.ShapeDtypeStruct(values.shape, F32),
            jax.ShapeDtypeStruct(anchor.shape, jnp.int32),
            jax.ShapeDtypeStruct(owner.shape, jnp.int32),
        ),
        in_specs=[HBM] * 6,
        out_specs=(VMEM,) * 6,
        scratch_shapes=[
            pltpu.VMEM(lagrange.shape, F32),
            pltpu.VMEM(filtered.shape, F32),
            pltpu.VMEM(filtered.shape, F32),
            pltpu.SemaphoreType.DMA((6,)),
        ],
        compiler_params=params(4),
    )(*[in_hbm(t) for t in (values, anchor, owner, lagrange, filtered, sensitivity)])


def bucket_kernel(chunks, values_ref, anchor_ref, owner_ref, out_ref):
    rows = values_ref.shape[0]
    owners = out_ref.shape[0]
    owner = owner_ref[...]
    anchor = anchor_ref[...]
    place = (anchor // (8 * chunks)) * (8 * chunks) + (anchor % chunks) * 8 + (anchor // chunks) % 8
    down = iota((rows, rows), 0)
    across = iota((rows, rows), 1)
    owner_f = owner.astype(F32)
    owner_column = jnp.sum(
        jnp.where(down == across, jnp.broadcast_to(owner_f, (rows, rows)), 0.0), axis=1, keepdims=True
    )
    earlier = (owner_column == owner_f) & (down < across)
    rank = jnp.sum(jnp.where(earlier, 1.0, 0.0), axis=0, keepdims=True)
    slot = iota((owners * CAP, rows), 0)
    chosen = jnp.where((slot // CAP == owner) & ((slot % CAP).astype(F32) == rank), 1.0, 0.0)
    named = jnp.where(iota((owners, rows), 0) == owner, 1.0, 0.0)
    lane = iota((LANES, rows), 0)
    marked = jnp.where((lane % CAP).astype(F32) == rank, place.astype(F32) + 1.0, 0.0)
    anchors = lax.dot_general(
        named, marked, (((1,), (1,)), ((), ())), precision=HIGHEST, preferred_element_type=F32
    )
    lower = (anchors.astype(jnp.int32) - 1) % 8 < 4
    blank = jnp.zeros((1, LANES), F32)
    from_next = jnp.concatenate([jnp.where(lower, anchors, 0.0)[1:], blank], axis=0)
    from_last = jnp.concatenate([blank, jnp.where(lower, 0.0, anchors)[:-1]], axis=0)
    for i, line in enumerate((anchors, from_next, from_last)):
        out_ref[:, 3 * CAP + i, :] = line
    packed = jnp.dot(chosen, values_ref[...], precision=HIGHEST, preferred_element_type=F32)
    packed = packed.reshape(owners, CAP, LANES)
    nothing = jnp.zeros((1, CAP, LANES), F32)
    out_ref[:, 0:CAP, :] = packed
    out_ref[0 : owners - 1, CAP : 2 * CAP, :] = packed[1:]
    out_ref[owners - 1 :, CAP : 2 * CAP, :] = nothing
    out_ref[1:, 2 * CAP : 3 * CAP, :] = packed[:-1]
    out_ref[0:1, 2 * CAP : 3 * CAP, :] = nothing


def bucket(values, anchor, owner, owners, chunks):
    return pl.pallas_call(
        functools.partial(bucket_kernel, chunks),
        out_shape=jax.ShapeDtypeStruct((owners, 4 * CAP, LANES), F32),
        in_specs=[VMEM] * 3,
        out_specs=VMEM,
        compiler_params=params(4),
    )(values, anchor, owner)


def exact_parts(values):
    top = values.astype(BF16)
    rest = values - top.astype(F32)
    middle = rest.astype(BF16)
    last = (rest - middle.astype(F32)).astype(BF16)
    return jnp.concatenate([top, middle, last], axis=1)


def scatter(recv_ref, own, beside, layers, layer_rows):
    owners = recv_ref.shape[0]
    group = min(LANES // CAP, owners)
    peer = iota((owners, LANES), 0)
    lane = iota((owners, LANES), 1)

    def places(line):
        kept = jnp.where(lane // CAP == peer % group, recv_ref[:, line, :], 0.0)
        sums = [jnp.sum(kept[g : g + group], axis=0, keepdims=True) for g in range(0, owners, group)]
        return [t[:, : group * CAP] for t in sums]

    def slots(start):
        return recv_ref[:, start : start + CAP, :].reshape(owners * CAP, LANES)

    for ref, lines, starts in ((own, (24,), (0,)), (beside, (25, 26), (8, 16))):
        anchors = jnp.concatenate([p for line in lines for p in places(line)], axis=1)
        parts = jnp.concatenate([exact_parts(slots(start)) for start in starts], axis=0)
        for first in layers:
            start, step = first * layer_rows, HALO * layer_rows
            row = (iota((step, anchors.shape[1]), 0) + (start + 1)).astype(F32)
            hot = jnp.where(row == anchors, 1.0, 0.0).astype(BF16)
            added = jnp.dot(hot, parts, preferred_element_type=F32)
            ref[start : start + step, :] = (
                added[:, 0:LANES] + added[:, LANES : 2 * LANES] + added[:, 2 * LANES : 3 * LANES]
            )


def tall_tiles(half, inner, outer):
    return pltpu.roll(jnp.where(half, inner, outer), 4, 0), pltpu.roll(jnp.where(half, outer, inner), 4, 0)


def halo_tile(half, odd, low, high):
    return pltpu.roll(jnp.where(half, high, low), 4, 0) if odd else jnp.where(half, low, high)


def tall_row(x, c, chunks):
    return GUARD + ((x + HALO) * chunks + c) * TALL


def face_rows(chunks):
    to = 0
    for d, count in zip(range(HALO, 0, -1), FACE_ROWS):
        skip = (TALL - count) // 2
        for c in range(chunks):
            for more in sorted({0, count - 8}):
                yield c, d, c // 2, (c % 2) * FACE + to + more, skip + more
        to += count


def fill_faces(s_ref, low_ref, high_ref, width_x, chunks):
    for c, d, page, line, skip in face_rows(chunks):
        for ref, x in ((low_ref, d - 1), (high_ref, width_x - d)):
            row = tall_row(x, c, chunks) + skip
            ref[page, line : line + 8, :] = s_ref[pl.ds(row, 8), :]


def read_faces(s_ref, left_ref, right_ref, masks_ref, width_x, chunks):
    for c, d, page, line, skip in face_rows(chunks):
        for ref, x, keep in ((left_ref, -d, masks_ref[LEFT]), (right_ref, width_x - 1 + d, masks_ref[RIGHT])):
            row = tall_row(x, c, chunks) + skip
            s_ref[pl.ds(row, 8), :] = ref[page, line : line + 8, :] * keep


def extended(shape):
    width_x, width_y, width_z = shape
    return jax.ShapeDtypeStruct(((width_x + 2 * HALO) * (width_z // LANES) * TALL + 2 * GUARD, LANES), F32)


def face_shape(shape):
    return jax.ShapeDtypeStruct((shape[2] // LANES // 2, 2 * FACE, LANES), F32)


def slope_kernel(
    filtered_hbm, above_ref, below_ref, masks_ref, s_ref, low_ref, high_ref, volume_ref, filtered_ref, sems
):
    (copy,) = start_all(((filtered_hbm, filtered_ref),), sems)
    width_x, width_y, width_z = filtered_ref.shape
    chunks = width_z // LANES
    edge = jnp.tanh(jnp.full((8, LANES), 4.0, F32))
    inverse = 1.0 / (edge + edge)
    eight = 8.0 * inverse
    half = iota((width_y, LANES), 0) < 4
    rim = masks_ref[RIM_HALO] * eight

    copy.wait()
    total = jnp.zeros((8, LANES), F32)
    for i, c in itertools.product(range(width_x // 2), range(chunks)):
        at = pl.ds(c * LANES, LANES)
        low, high = above_ref[0, i, :, at], below_ref[0, i, :, at]
        for odd in range(2):
            x = 2 * i + odd
            part = jnp.tanh(8.0 * (filtered_ref[x, :, at] - 0.5))
            total = total + (edge + part) * inverse
            side = jnp.tanh(8.0 * (halo_tile(half, odd, low, high) - 0.5))
            tiles = tall_tiles(half, (1.0 - part * part) * eight, (1.0 - side * side) * rim)
            row = tall_row(x, c, chunks)
            s_ref[pl.ds(row, 8), :] = tiles[0]
            s_ref[pl.ds(row + 8, 8), :] = tiles[1]
    volume_ref[...] = total
    fill_faces(s_ref, low_ref, high_ref, width_x, chunks)


def make_slope(filtered, above, below, masks):
    face = face_shape(filtered.shape)
    return pl.pallas_call(
        slope_kernel,
        out_shape=(extended(filtered.shape), face, face, jax.ShapeDtypeStruct((8, LANES), F32)),
        in_specs=[HBM] + [VMEM] * 3,
        out_specs=(VMEM,) * 4,
        scratch_shapes=[pltpu.VMEM(filtered.shape, F32), pltpu.SemaphoreType.DMA((1,))],
        compiler_params=params(4),
        cost_estimate=pl.CostEstimate(flops=4_000_000, bytes_accessed=4_000_000, transcendentals=300_000),
    )(in_hbm(filtered), above, below, masks)


def source_pair(i, s_ref, slope_ref, sensitivity_ref, above_ref, below_ref, own, beside, masks_ref):
    width_x, width_y, width_z = sensitivity_ref.shape
    chunks = width_z // LANES
    base = masks_ref[BASE]
    half = iota((width_y, LANES), 0) < 4
    for c in range(chunks):
        at = pl.ds(c * LANES, LANES)
        low, high = above_ref[1, i, :, at], below_ref[1, i, :, at]
        for odd in range(2):
            x = 2 * i + odd
            line = pl.ds((x * chunks + c) * 8, 8)
            inner = sensitivity_ref[x, :, at] + own[line, :]
            outer = halo_tile(half, odd, low, high) + beside[line, :]
            row = tall_row(x, c, chunks)
            for t, tile in enumerate(tall_tiles(half, inner, outer)):
                rows = pl.ds(row + 8 * t, 8)
                s_ref[rows, :] = slope_ref[rows, :] * (tile + base)


def edge_kernel(
    recv_ref, sensitivity_hbm, above_ref, below_ref, slope_ref, masks_ref,
    s_ref, low_ref, high_ref, own, beside, sensitivity_ref, sems,
):
    width_x, width_y, width_z = sensitivity_ref.shape
    parts = [pl.ds(x, HALO) for x in (0, width_x - HALO)]
    copies = start_all([(sensitivity_hbm.at[part], sensitivity_ref.at[part]) for part in parts], sems)
    chunks = width_z // LANES
    scatter(recv_ref, own, beside, (0, width_x - HALO), width_y * chunks)
    for copy in copies:
        copy.wait()
    for i in (*range(HALO // 2), *range((width_x - HALO) // 2, width_x // 2)):
        source_pair(i, s_ref, slope_ref, sensitivity_ref, above_ref, below_ref, own, beside, masks_ref)
    fill_faces(s_ref, low_ref, high_ref, width_x, chunks)


def make_edges(recv, sensitivity, above, below, slope, masks):
    width_x, width_y, width_z = sensitivity.shape
    face = face_shape(sensitivity.shape)
    scratch = pltpu.VMEM((width_x * width_y * width_z // LANES, LANES), F32)
    return pl.pallas_call(
        edge_kernel,
        out_shape=(extended(sensitivity.shape), face, face),
        in_specs=[VMEM, HBM] + [VMEM] * 4,
        out_specs=(VMEM,) * 3,
        scratch_shapes=[scratch] * 2 + [pltpu.VMEM(sensitivity.shape, F32), pltpu.SemaphoreType.DMA((2,))],
        compiler_params=params(8),
    )(recv, in_hbm(sensitivity), above, below, slope, masks)


def weight_of(k):
    return (25.0 / 4.0) ** k / 25.0


def sweep(ref, source, base, k, chunks):
    layer = chunks * TALL
    lane = iota((8, LANES), 1)
    own = [ref[pl.ds(base + c * TALL, 8), :] for c in range(chunks)]
    up = [pltpu.roll(t, LANES - 1, 1) for t in own]
    down = [pltpu.roll(t, 1, 1) for t in own]
    zero = jnp.zeros((8, LANES), F32)
    results = []
    for c in range(chunks):
        at = base + c * TALL
        total = jnp.where(lane == LANES - 1, up[c + 1] if c + 1 < chunks else zero, up[c])
        total = total + jnp.where(lane == 0, down[c - 1] if c else zero, down[c])
        total = total + (ref[pl.ds(at - 1, 8), :] + ref[pl.ds(at + 1, 8), :])
        total = total + (ref[pl.ds(at - layer, 8), :] + ref[pl.ds(at + layer, 8), :])
        results.append(total + weight_of(k) * source[pl.ds(at, 8), :])
    return results


def sweep_layer(old, new, source, x, k, rims, keep, chunks):
    for tile in range(2):
        mask = rims[tile] if keep is None else rims[tile] * keep
        base = tall_row(x, 0, chunks) + 8 * tile
        for c, value in enumerate(sweep(old, source, base, k, chunks)):
            new[pl.ds(base + c * TALL, 8), :] = value * mask


def last_layer(old, source, x, chunks):
    scale = (4.0 / 25.0) ** SWEEPS
    return [scale * t for t in sweep(old, source, tall_row(x, 0, chunks) + HALO, SWEEPS, chunks)]


def store_layer(ref, x, values):
    for c, value in enumerate(values):
        ref[x, :, pl.ds(c * LANES, LANES)] = value


def load_layer(ref, x, chunks):
    return [ref[x, :, pl.ds(c * LANES, LANES)] for c in range(chunks)]


def add_products(total, left, right):
    for a, b in zip(left, right):
        total = total + a * b
    return total


def zero_tile():
    return jnp.zeros((8, LANES), F32)


def inner_sweeps(refs, masks_ref, width_x, chunks):
    rims = (masks_ref[RIM], masks_ref[RIM + 1])
    for k in range(1, SWEEPS):
        for x in range(k, width_x - k):
            sweep_layer(refs[k - 1], refs[k], refs[0], x, k, rims, None, chunks)
    return [last_layer(refs[SWEEPS - 1], refs[0], x, chunks) for x in range(HALO, width_x - HALO)]


def outer_sweeps(refs, masks_ref, width_x, chunks):
    rims = (masks_ref[RIM], masks_ref[RIM + 1])
    for k in range(1, SWEEPS):
        for x in range(k - HALO, k):
            sweep_layer(refs[k - 1], refs[k], refs[0], x, k, rims, masks_ref[LEFT] if x < 0 else None, chunks)
            x = width_x - 1 - x
            keep = masks_ref[RIGHT] if x >= width_x else None
            sweep_layer(refs[k - 1], refs[k], refs[0], x, k, rims, keep, chunks)
    layers = (*range(HALO), *range(width_x - HALO, width_x))
    return [last_layer(refs[SWEEPS - 1], refs[0], x, chunks) for x in layers]


def half_block(shape):
    return jax.ShapeDtypeStruct((shape[0] - 2 * HALO,) + shape[1:], F32), jax.ShapeDtypeStruct(
        (2 * HALO,) + shape[1:], F32
    )


TILE = jax.ShapeDtypeStruct((8, LANES), F32)


def slope_inner_kernel(width_x, s_ref, masks_ref, one, two, three, raw_ref, square_ref):
    chunks = raw_ref.shape[2] // LANES
    total = zero_tile()
    for i, values in enumerate(inner_sweeps((s_ref, one, two, three), masks_ref, width_x, chunks)):
        store_layer(raw_ref, i, values)
        total = add_products(total, values, values)
    square_ref[...] = total


def make_slope_inner(s, masks, shape):
    wide = extended(shape)
    return pl.pallas_call(
        functools.partial(slope_inner_kernel, shape[0]),
        out_shape=(wide, wide, wide, half_block(shape)[0], TILE),
        in_specs=[VMEM] * 2,
        out_specs=(VMEM,) * 5,
        compiler_params=params(2),
        cost_estimate=pl.CostEstimate(flops=15_000_000, bytes_accessed=8_000_000, transcendentals=0),
    )(s, masks)


def slope_outer_kernel(
    width_x, left_ref, right_ref, masks_ref, inner_square_ref, s_in, one_in, two_in, three_in,
    one, two, three, raw_ref, square_ref, s_ref,
):
    del one_in, two_in, three_in
    chunks = raw_ref.shape[2] // LANES
    for x in (0, width_x - HALO):
        rows = pl.ds(tall_row(x, 0, chunks), HALO * chunks * TALL)
        s_ref[rows, :] = s_in[rows, :]
    read_faces(s_ref, left_ref, right_ref, masks_ref, width_x, chunks)
    total = inner_square_ref[...]
    for i, values in enumerate(outer_sweeps((s_ref, one, two, three), masks_ref, width_x, chunks)):
        store_layer(raw_ref, i, values)
        total = add_products(total, values, values)
    square_ref[...] = total


def make_slope_outer(left, right, masks, square, s, wide, shape):
    same = jax.ShapeDtypeStruct(s.shape, F32)
    return pl.pallas_call(
        functools.partial(slope_outer_kernel, shape[0]),
        out_shape=(same, same, same, half_block(shape)[1], TILE),
        in_specs=[VMEM] * 8,
        out_specs=(VMEM,) * 5,
        input_output_aliases={5: 0, 6: 1, 7: 2},
        scratch_shapes=[pltpu.VMEM(s.shape, F32)],
        compiler_params=params(4),
        cost_estimate=pl.CostEstimate(flops=10_000_000, bytes_accessed=6_000_000, transcendentals=0),
    )(left, right, masks, square, s, *wide)[3:]


def source_inner_kernel(
    recv_ref, sensitivity_hbm, above_ref, below_ref, slope_ref, masks_ref, slope_raw_ref,
    design_hbm, first_hbm, second_hbm, edges_ref,
    s_ref, one, two, three, raw_ref, sums_ref, design_ref, first_ref, second_ref, own, beside, sensitivity_ref, sems,
):
    del edges_ref
    width_x, width_y, width_z = sensitivity_ref.shape
    chunks = width_z // LANES
    part = pl.ds(HALO, width_x - 2 * HALO)
    copies = start_all(
        (
            (sensitivity_hbm.at[part], sensitivity_ref.at[part]),
            (design_hbm, design_ref),
            (first_hbm, first_ref),
            (second_hbm, second_ref),
        ),
        sems,
    )
    scatter(recv_ref, own, beside, range(HALO, width_x - HALO, HALO), width_y * chunks)
    copies[0].wait()
    for i in range(HALO // 2, (width_x - HALO) // 2):
        source_pair(i, s_ref, slope_ref, sensitivity_ref, above_ref, below_ref, own, beside, masks_ref)
    aa, ab = zero_tile(), zero_tile()
    for i, values in enumerate(inner_sweeps((s_ref, one, two, three), masks_ref, width_x, chunks)):
        store_layer(raw_ref, i, values)
        aa = add_products(aa, values, values)
        ab = add_products(ab, values, load_layer(slope_raw_ref, i, chunks))
    sums_ref[0] = aa
    sums_ref[1] = ab
    for copy in copies[1:]:
        copy.wait()


def make_source_inner(
    recv, sensitivity, above, below, slope, masks, slope_raw, design, first_moment, second_moment, edges
):
    block = jax.ShapeDtypeStruct(design.shape, F32)
    wide = extended(design.shape)
    scratch = pltpu.VMEM((design.size // LANES, LANES), F32)
    return pl.pallas_call(
        source_inner_kernel,
        out_shape=(wide,) * 4
        + (half_block(design.shape)[0], jax.ShapeDtypeStruct((2, 8, LANES), F32))
        + (block,) * 3,
        in_specs=[VMEM, HBM] + [VMEM] * 5 + [HBM] * 3 + [VMEM],
        out_specs=(VMEM,) * 9,
        input_output_aliases={10: 0},
        scratch_shapes=[scratch] * 2 + [pltpu.VMEM(design.shape, F32), pltpu.SemaphoreType.DMA((4,))],
        compiler_params=params(8),
        cost_estimate=pl.CostEstimate(flops=40_000_000, bytes_accessed=16_000_000, transcendentals=0),
    )(
        recv, in_hbm(sensitivity), above, below, slope, masks, slope_raw,
        in_hbm(design), in_hbm(first_moment), in_hbm(second_moment), edges,
    )


def source_outer_kernel(
    width_x, left_ref, right_ref, masks_ref, slope_raw_ref, volume_ref, sums_ref, square_ref,
    s_in, one_in, two_in, three_in,
    s_ref, one, two, three, raw_ref, send_ref,
):
    del s_in, one_in, two_in, three_in
    chunks = raw_ref.shape[2] // LANES
    read_faces(s_ref, left_ref, right_ref, masks_ref, width_x, chunks)
    aa, ab = sums_ref[0], sums_ref[1]
    for i, values in enumerate(outer_sweeps((s_ref, one, two, three), masks_ref, width_x, chunks)):
        store_layer(raw_ref, i, values)
        aa = add_products(aa, values, values)
        ab = add_products(ab, values, load_layer(slope_raw_ref, i, chunks))
    lane = iota((1, LANES), 1)
    line = jnp.zeros((1, LANES), F32)
    for i, tile in enumerate((volume_ref[...], aa, ab, square_ref[...])):
        total = jnp.sum(tile, axis=0, keepdims=True)
        total = total + pltpu.roll(total, LANES // 2, 1)
        total = total + pltpu.roll(total, LANES // 4, 1)
        line = jnp.where(lane // (LANES // 4) == i, total, line)
    send_ref[...] = jnp.broadcast_to(line, send_ref.shape)


def make_source_outer(left, right, masks, slope_raw, volume, sums, square, wide, copies, shape):
    same = jax.ShapeDtypeStruct(wide[0].shape, F32)
    return pl.pallas_call(
        functools.partial(source_outer_kernel, shape[0]),
        out_shape=(same,) * 4 + (half_block(shape)[1], jax.ShapeDtypeStruct((copies, LANES), F32)),
        in_specs=[VMEM] * 11,
        out_specs=(VMEM,) * 6,
        input_output_aliases={7: 0, 8: 1, 9: 2, 10: 3},
        compiler_params=params(4),
    )(left, right, masks, slope_raw, volume, sums, square, *wide)[4:]


def adam_kernel(
    cells, sums_ref, masks_ref, inner_ref, outer_ref, slope_inner_ref, slope_outer_ref, design_ref, first_ref, second_ref,
    d_hbm, m_hbm, v_hbm, g_hbm, d_ref, m_ref, v_ref, g_ref, sems,
):
    width_x = design_ref.shape[0]
    line = jnp.sum(sums_ref[...], axis=0, keepdims=True)
    part = iota(line.shape, 1) // (LANES // 4)

    def picked(scale):
        return jnp.sum(line * scale, axis=1, keepdims=True)

    volume = picked(jnp.where(part == 0, 1.0, 0.0))
    shift = masks_ref[PENALTY, 0:1, 0:1] * (volume / cells / 0.4 - 1.25)
    total = picked(
        jnp.where(part == 1, 1.0, jnp.where(part == 2, 2.0 * shift, jnp.where(part == 3, shift * shift, 0.0)))
    )
    inverse = 1.0 / jnp.sqrt(jnp.maximum(total, 0.0) / cells + 1e-06)
    blocks = width_x // HALO
    copies = []
    for block in range(blocks):
        part = pl.ds(block * HALO, HALO)
        if block in (0, blocks - 1):
            raw, slope_raw, start = outer_ref, slope_outer_ref, 0 if block == 0 else HALO
        else:
            raw, slope_raw, start = inner_ref, slope_inner_ref, (block - 1) * HALO
        for i in range(HALO):
            x = block * HALO + i
            gradient = (raw[start + i] + shift * slope_raw[start + i]) * inverse
            new_first = 0.9 * first_ref[x] + 0.1 * gradient
            new_second = 0.999 * second_ref[x] + 0.001 * gradient * gradient
            first_hat = new_first * (0.05 / (1.0 - 0.9**ADAM_STEP))
            second_hat = new_second * (1.0 / (1.0 - 0.999**ADAM_STEP))
            d_ref[x] = jnp.clip(design_ref[x] - first_hat / (jnp.sqrt(second_hat) + 1e-08), 0.0, 1.0)
            m_ref[x] = new_first
            v_ref[x] = new_second
            g_ref[x] = gradient
        for i, (ref, hbm) in enumerate(((d_ref, d_hbm), (m_ref, m_hbm), (v_ref, v_hbm), (g_ref, g_hbm))):
            copy = pltpu.make_async_copy(ref.at[part], hbm.at[part], sems.at[block, i])
            copy.start()
            copies.append(copy)
    for copy in copies:
        copy.wait()


def adam(cells, sums, masks, parts, design, first_moment, second_moment):
    return pl.pallas_call(
        functools.partial(adam_kernel, cells),
        out_shape=(jax.ShapeDtypeStruct(design.shape, F32),) * 4,
        in_specs=[VMEM] * 9,
        out_specs=(HBM,) * 4,
        scratch_shapes=[pltpu.VMEM(design.shape, F32)] * 4 + [pltpu.SemaphoreType.DMA((4, 4))],
        compiler_params=params(6),
    )(sums, masks, *parts, design, first_moment, second_moment)


def shift(cells, axis, by):
    count = lax.axis_size(axis)
    return lax.ppermute(cells, axis, [(i, (i + by) % count) for i in range(count)])


def per_device(
    design,
    filtered,
    sensitivity,
    first_moment,
    second_moment,
    lagrange,
    trace_values,
    trace_anchor,
    trace_owner,
):
    width_x, width_y, depth = design.shape
    count_x, count_y = lax.axis_size("gx"), lax.axis_size("gy")
    cells = float(width_x * width_y * depth * count_x * count_y)
    rows = trace_values.shape[1]
    low, high, masks, *trace = make_first(
        trace_values[0], trace_anchor, trace_owner.reshape(1, rows), lagrange.reshape(1, 2), filtered, sensitivity
    )
    below, above = shift(high, "gy", 1), shift(low, "gy", -1)
    received = lax.all_to_all(bucket(*trace, count_y, depth // LANES), "gy", 0, 0, tiled=True)

    slope, low, high, volume = make_slope(filtered, above, below, masks)
    left, right = shift(high, "gx", 1), shift(low, "gx", -1)
    shape = design.shape
    *wide, slope_inner, square = make_slope_inner(slope, masks, shape)
    slope_outer, square = make_slope_outer(left, right, masks, square, slope, wide, shape)

    source, low, high = make_edges(received, sensitivity, above, below, slope, masks)
    left, right = shift(high, "gx", 1), shift(low, "gx", -1)
    *wide, inner, sums, design, first_moment, second_moment = make_source_inner(
        received, sensitivity, above, below, slope, masks, slope_inner, design, first_moment, second_moment, source
    )
    outer, sums = make_source_outer(
        left, right, masks, slope_outer, volume, sums, square, wide, count_x * count_y, shape
    )
    sums = lax.all_to_all(sums, ("gx", "gy"), 0, 0, tiled=True)
    parts = (inner, outer, slope_inner, slope_outer)
    return adam(cells, sums, masks, parts, design, first_moment, second_moment)


def solution(mesh):
    block = P("gx", "gy", None)
    return jax.shard_map(
        per_device,
        mesh=mesh,
        in_specs=(block, block, block, block, block, P(), block, P("gx", "gy"), block),
        out_specs=(block, block, block, block),
        check_vma=False,
    )
```

```python
import functools
import itertools

import jax
import jax.numpy as jnp
from jax import lax
from jax.experimental import pallas as pl
from jax.experimental.pallas import tpu as pltpu
from jax.sharding import PartitionSpec as P

SWEEPS = 4
ADAM_STEP = 10
CAP = 8
LANES = 128
HALO = 4
TALL = 16
GUARD = 8
FACE_ROWS = (8, 10, 12, 14)
FACE = sum(FACE_ROWS)
SENT = 3 * CAP + 1
GROUPS = LANES // CAP
LISTS = 5
LEFT, RIGHT, RIM, RIM_HALO, BASE, PENALTY = 0, 1, 2, 4, 5, 6
F32 = jnp.float32
BF16 = jnp.bfloat16
MIB = 1024 * 1024


def params(mib):
    return pltpu.CompilerParams(vmem_limit_bytes=mib * MIB)


VMEM = pl.BlockSpec(memory_space=pltpu.VMEM)
HBM = pl.BlockSpec(memory_space=pltpu.HBM)


def iota(shape, dim):
    return lax.broadcasted_iota(jnp.int32, shape, dim)


def in_hbm(array):
    return pltpu.with_memory_space_constraint(array, pltpu.HBM)


def start_all(pairs, sems):
    copies = [pltpu.make_async_copy(src, dst, sems.at[i]) for i, (src, dst) in enumerate(pairs)]
    for copy in copies:
        copy.start()
    return copies


def exact_parts(values):
    top = values.astype(BF16)
    rest = values - top.astype(F32)
    middle = rest.astype(BF16)
    last = (rest - middle.astype(F32)).astype(BF16)
    return jnp.concatenate([top, middle, last], axis=1)


def bucket_rows(values, anchor, owner, owners, chunks):
    rows = values.shape[0]
    place = (anchor // (8 * chunks)) * (8 * chunks) + (anchor % chunks) * 8 + (anchor // chunks) % 8
    down = iota((rows, rows), 0)
    across = iota((rows, rows), 1)
    owner_f = owner.astype(F32)
    owner_column = jnp.sum(
        jnp.where(down == across, jnp.broadcast_to(owner_f, (rows, rows)), 0.0), axis=1, keepdims=True
    )
    earlier = (owner_column == owner_f) & (down < across)
    rank = jnp.sum(jnp.where(earlier, 1.0, 0.0), axis=0, keepdims=True)
    slot = iota((owners * CAP, rows), 0)
    chosen = jnp.where((slot // CAP == owner) & ((slot % CAP).astype(F32) == rank), 1.0, 0.0).astype(BF16)
    added = jnp.dot(chosen, exact_parts(values), preferred_element_type=F32)
    packed = added[:, 0:LANES] + added[:, LANES : 2 * LANES] + added[:, 2 * LANES : 3 * LANES]
    named = jnp.where(iota((owners, rows), 0) == owner, 1.0, 0.0).astype(BF16)
    number = place + 1
    ranked = (iota((LANES, rows), 0) % CAP).astype(F32) == rank
    marked = jnp.concatenate(
        [jnp.where(ranked, t.astype(F32), 0.0).astype(BF16) for t in (number // 32, number % 32)], axis=0
    )
    found = lax.dot_general(named, marked, (((1,), (1,)), ((), ())), preferred_element_type=F32)
    return packed, 32.0 * found[:, 0:LANES] + found[:, LANES : 2 * LANES]


def first_kernel(
    values_hbm, anchor_hbm, owner_hbm, lagrange_hbm, filtered_hbm, sensitivity_hbm,
    low_ref, high_ref, masks_ref, packed_ref, anchors_ref,
    values_ref, anchor_ref, owner_ref, lagrange_ref, filtered_ref, sensitivity_ref, sems,
):
    copies = start_all(
        (
            (anchor_hbm, anchor_ref),
            (owner_hbm, owner_ref),
            (values_hbm, values_ref),
            (lagrange_hbm, lagrange_ref),
            (filtered_hbm, filtered_ref),
            (sensitivity_hbm, sensitivity_ref),
        ),
        sems,
    )
    width_x, width_y, width_z = filtered_ref.shape
    index_x, index_y = lax.axis_index("gx"), lax.axis_index("gy")
    one, zero = jnp.ones((8, LANES), F32), jnp.zeros((8, LANES), F32)
    upper = iota((8, LANES), 0) < 4
    before, after = jnp.where(index_y > 0, one, zero), jnp.where(index_y < lax.axis_size("gy") - 1, one, zero)
    masks_ref[LEFT] = jnp.where(index_x > 0, one, zero)
    masks_ref[RIGHT] = jnp.where(index_x < lax.axis_size("gx") - 1, one, zero)
    masks_ref[RIM] = jnp.where(upper, before, one)
    masks_ref[RIM + 1] = jnp.where(upper, one, after)
    masks_ref[RIM_HALO] = jnp.where(upper, after, before)
    for copy in copies[:4]:
        copy.wait()
    weight, penalty = lagrange_ref[0:1, 0:1], lagrange_ref[0:1, 1:2]
    masks_ref[BASE] = one * (weight + 0.25 * penalty)
    masks_ref[PENALTY] = one * penalty
    packed_ref[...], anchors_ref[...] = bucket_rows(
        values_ref[...], anchor_ref[...], owner_ref[...], anchors_ref.shape[0], width_z // LANES
    )
    half = iota((width_y, width_z), 0) < 4
    for f, ref in enumerate((filtered_ref, sensitivity_ref)):
        copies[4 + f].wait()
        for i in range(width_x // 2):
            even, odd = ref[2 * i], pltpu.roll(ref[2 * i + 1], 4, 0)
            low_ref[f, i] = jnp.where(half, even, odd)
            high_ref[f, i] = jnp.where(half, odd, even)


def make_first(values, anchor, owner, lagrange, filtered, sensitivity, owners):
    width_x, width_y, width_z = filtered.shape
    face = jax.ShapeDtypeStruct((2, width_x // 2, width_y, width_z), F32)
    return pl.pallas_call(
        first_kernel,
        out_shape=(
            face,
            face,
            jax.ShapeDtypeStruct((7, 8, LANES), F32),
            jax.ShapeDtypeStruct((owners * CAP, LANES), F32),
            jax.ShapeDtypeStruct((owners, LANES), F32),
        ),
        in_specs=[HBM] * 6,
        out_specs=(VMEM,) * 5,
        scratch_shapes=[
            pltpu.VMEM(values.shape, F32),
            pltpu.VMEM(anchor.shape, jnp.int32),
            pltpu.VMEM(owner.shape, jnp.int32),
            pltpu.VMEM(lagrange.shape, F32),
            pltpu.VMEM(filtered.shape, F32),
            pltpu.VMEM(filtered.shape, F32),
            pltpu.SemaphoreType.DMA((6,)),
        ],
        compiler_params=params(8),
    )(*[in_hbm(t) for t in (values, anchor, owner, lagrange, filtered, sensitivity)])


def send_kernel(packed_ref, anchors_ref, out_ref):
    owners = anchors_ref.shape[0]
    anchors = anchors_ref[...]
    lower = (anchors.astype(jnp.int32) - 1) % 8 < 4
    blank = jnp.zeros((1, LANES), F32)
    from_next = jnp.concatenate([jnp.where(lower, anchors, 0.0)[1:], blank], axis=0)
    from_last = jnp.concatenate([blank, jnp.where(lower, 0.0, anchors)[:-1]], axis=0)
    group = iota((owners, LANES), 1) // CAP
    me = lax.axis_index("gy")
    line = jnp.zeros((owners, LANES), F32)
    for i, part in enumerate((anchors, from_next, from_last)):
        line = jnp.where(group == (me + i * LISTS) % GROUPS, part, line)
    nothing = jnp.zeros((CAP, LANES), F32)
    for b in range(owners):
        for i, near in enumerate((b, b + 1, b - 1)):
            rows = packed_ref[near * CAP : (near + 1) * CAP, :] if 0 <= near < owners else nothing
            out_ref[b * SENT + i * CAP : b * SENT + (i + 1) * CAP, :] = rows
        out_ref[(b + 1) * SENT - 1 : (b + 1) * SENT, :] = line[b : b + 1]


def make_send(packed, anchors):
    return pl.pallas_call(
        send_kernel,
        out_shape=jax.ShapeDtypeStruct((anchors.shape[0] * SENT, LANES), F32),
        in_specs=[VMEM] * 2,
        out_specs=VMEM,
        compiler_params=params(8),
    )(packed, anchors)


def scatter(recv_ref, own, beside, layers, layer_rows):
    owners = recv_ref.shape[0] // SENT
    lines = recv_ref[pl.ds(SENT - 1, owners, stride=SENT), :]
    peer = iota((owners, LANES), 0)
    group = iota((owners, LANES), 1) // CAP

    def places(i):
        kept = jnp.where(group == (peer + i * LISTS) % GROUPS, lines, 0.0)
        sums = [jnp.sum(kept[g : g + GROUPS], axis=0, keepdims=True) for g in range(0, owners, GROUPS)]
        return [pltpu.roll(t, LANES - i * LISTS * CAP, 1) for t in sums] if i else sums

    def slots(i):
        return jnp.concatenate(
            [recv_ref[p * SENT + i * CAP : p * SENT + (i + 1) * CAP, :] for p in range(owners)], axis=0
        )

    for ref, lists in ((own, (0,)), (beside, (1, 2))):
        anchors = jnp.concatenate([t for i in lists for t in places(i)], axis=1)
        parts = jnp.concatenate([exact_parts(slots(i)) for i in lists], axis=0)
        for first in layers:
            start, step = first * layer_rows, HALO * layer_rows
            row = (iota((step, anchors.shape[1]), 0) + (start + 1)).astype(F32)
            hot = jnp.where(row == anchors, 1.0, 0.0).astype(BF16)
            added = jnp.dot(hot, parts, preferred_element_type=F32)
            ref[start : start + step, :] = (
                added[:, 0:LANES] + added[:, LANES : 2 * LANES] + added[:, 2 * LANES : 3 * LANES]
            )


def tall_tiles(half, inner, outer):
    return pltpu.roll(jnp.where(half, inner, outer), 4, 0), pltpu.roll(jnp.where(half, outer, inner), 4, 0)


def halo_tile(half, odd, low, high):
    return pltpu.roll(jnp.where(half, high, low), 4, 0) if odd else jnp.where(half, low, high)


def tall_row(x, c, chunks):
    return GUARD + ((x + HALO) * chunks + c) * TALL


def flat_row(x, c, chunks):
    return (x * chunks + c) * TALL


def face_rows(chunks):
    to = 0
    for d, count in zip(range(HALO, 0, -1), FACE_ROWS):
        skip = (TALL - count) // 2
        for c in range(chunks):
            for more in sorted({0, count - 8}):
                yield c, d, c // 2, (c % 2) * FACE + to + more, skip + more
        to += count


def fill_faces(s_ref, low_ref, high_ref, width_x, chunks, row_of):
    for c, d, page, line, skip in face_rows(chunks):
        for ref, x in ((low_ref, d - 1), (high_ref, width_x - d)):
            row = row_of(x, c, chunks) + skip
            ref[page, line : line + 8, :] = s_ref[pl.ds(row, 8), :]


def read_faces(s_ref, left_ref, right_ref, masks_ref, width_x, chunks):
    for c, d, page, line, skip in face_rows(chunks):
        for ref, x, keep in ((left_ref, -d, masks_ref[LEFT]), (right_ref, width_x - 1 + d, masks_ref[RIGHT])):
            row = tall_row(x, c, chunks) + skip
            s_ref[pl.ds(row, 8), :] = ref[page, line : line + 8, :] * keep


def extended(shape):
    width_x, width_y, width_z = shape
    return jax.ShapeDtypeStruct(((width_x + 2 * HALO) * (width_z // LANES) * TALL + 2 * GUARD, LANES), F32)


def flat(shape):
    return jax.ShapeDtypeStruct((shape[0] * (shape[2] // LANES) * TALL, LANES), F32)


def face_shape(shape):
    return jax.ShapeDtypeStruct((shape[2] // LANES // 2, 2 * FACE, LANES), F32)


def slope_kernel(
    filtered_hbm, sensitivity_hbm, above_ref, below_ref, masks_ref,
    s_ref, base_ref, low_ref, high_ref, volume_ref, filtered_ref, sensitivity_ref, sems,
):
    copies = start_all(((filtered_hbm, filtered_ref), (sensitivity_hbm, sensitivity_ref)), sems)
    width_x, width_y, width_z = filtered_ref.shape
    chunks = width_z // LANES
    edge = jnp.tanh(jnp.full((8, LANES), 4.0, F32))
    inverse = 1.0 / (edge + edge)
    eight = 8.0 * inverse
    half = iota((width_y, LANES), 0) < 4
    rim = masks_ref[RIM_HALO] * eight
    base = masks_ref[BASE]
    for copy in copies:
        copy.wait()

    def pair(i, total):
        for c, odd in itertools.product(range(chunks), range(2)):
            at, x = pl.ds(c * LANES, LANES), 2 * i + odd
            part = jnp.tanh(8.0 * (filtered_ref[x, :, at] - 0.5))
            total = total + (edge + part) * inverse
            side, sense = [halo_tile(half, odd, above_ref[f, i, :, at], below_ref[f, i, :, at]) for f in range(2)]
            side = jnp.tanh(8.0 * (side - 0.5))
            row = pl.multiple_of(flat_row(x, c, chunks), 8)
            for t, tile in enumerate(tall_tiles(half, (1.0 - part * part) * eight, (1.0 - side * side) * rim)):
                s_ref[pl.ds(row + 8 * t, 8), :] = tile
            for t, tile in enumerate(tall_tiles(half, sensitivity_ref[x, :, at], sense)):
                base_ref[pl.ds(row + 8 * t, 8), :] = tile + base
        return total

    volume_ref[...] = lax.fori_loop(0, width_x // 2, pair, jnp.zeros((8, LANES), F32))
    fill_faces(s_ref, low_ref, high_ref, width_x, chunks, flat_row)


def make_slope(filtered, sensitivity, above, below, masks):
    face = face_shape(filtered.shape)
    rows = flat(filtered.shape)
    block = pltpu.VMEM(filtered.shape, F32)
    return pl.pallas_call(
        slope_kernel,
        out_shape=(rows, rows, face, face, jax.ShapeDtypeStruct((8, LANES), F32)),
        in_specs=[HBM] * 2 + [VMEM] * 3,
        out_specs=(VMEM,) * 5,
        scratch_shapes=[block, block, pltpu.SemaphoreType.DMA((2,))],
        compiler_params=params(8),
        cost_estimate=pl.CostEstimate(flops=4_000_000, bytes_accessed=4_000_000, transcendentals=300_000),
    )(in_hbm(filtered), in_hbm(sensitivity), above, below, masks)


def make_layers(layers, s_ref, slope_ref, base_ref, own, beside, chunks):
    half = iota((8, LANES), 0) < 4
    for x, c in itertools.product(layers, range(chunks)):
        line = pl.ds((x * chunks + c) * 8, 8)
        for t, tile in enumerate(tall_tiles(half, own[line, :], beside[line, :])):
            rows = pl.ds(flat_row(x, c, chunks) + 8 * t, 8)
            s_ref[pl.ds(tall_row(x, c, chunks) + 8 * t, 8), :] = slope_ref[rows, :] * (base_ref[rows, :] + tile)


def edge_kernel(width_x, recv_ref, base_ref, slope_ref, s_ref, low_ref, high_ref, own, beside):
    layer_rows = own.shape[0] // width_x
    chunks = layer_rows // 8
    scatter(recv_ref, own, beside, (0, width_x - HALO), layer_rows)
    layers = (*range(HALO), *range(width_x - HALO, width_x))
    make_layers(layers, s_ref, slope_ref, base_ref, own, beside, chunks)
    fill_faces(s_ref, low_ref, high_ref, width_x, chunks, tall_row)


def make_edges(recv, base, slope, shape):
    width_x, width_y, width_z = shape
    face = face_shape(shape)
    scratch = pltpu.VMEM((width_x * width_y * width_z // LANES, LANES), F32)
    return pl.pallas_call(
        functools.partial(edge_kernel, width_x),
        out_shape=(extended(shape), face, face),
        in_specs=[VMEM] * 3,
        out_specs=(VMEM,) * 3,
        scratch_shapes=[scratch] * 2,
        compiler_params=params(8),
    )(recv, base, slope)


def weight_of(k):
    return (25.0 / 4.0) ** k / 25.0


def sweep(ref, source, base, k, chunks):
    layer = chunks * TALL
    lane = iota((8, LANES), 1)
    own = [ref[pl.ds(base + c * TALL, 8), :] for c in range(chunks)]
    up = [pltpu.roll(t, LANES - 1, 1) for t in own]
    down = [pltpu.roll(t, 1, 1) for t in own]
    zero = jnp.zeros((8, LANES), F32)
    results = []
    for c in range(chunks):
        at = base + c * TALL
        total = jnp.where(lane == LANES - 1, up[c + 1] if c + 1 < chunks else zero, up[c])
        total = total + jnp.where(lane == 0, down[c - 1] if c else zero, down[c])
        total = total + (ref[pl.ds(at - 1, 8), :] + ref[pl.ds(at + 1, 8), :])
        total = total + (ref[pl.ds(at - layer, 8), :] + ref[pl.ds(at + layer, 8), :])
        results.append(total + weight_of(k) * source[pl.ds(at, 8), :])
    return results


def sweep_layer(old, new, source, x, k, rims, keep, chunks):
    for tile in range(2):
        mask = rims[tile] if keep is None else rims[tile] * keep
        base = tall_row(x, 0, chunks) + 8 * tile
        for c, value in enumerate(sweep(old, source, base, k, chunks)):
            new[pl.ds(base + c * TALL, 8), :] = value * mask


def last_layer(old, source, x, chunks):
    scale = (4.0 / 25.0) ** SWEEPS
    return [scale * t for t in sweep(old, source, tall_row(x, 0, chunks) + HALO, SWEEPS, chunks)]


def store_layer(ref, x, values):
    for c, value in enumerate(values):
        ref[x, :, pl.ds(c * LANES, LANES)] = value


def load_layer(ref, x, chunks):
    return [ref[x, :, pl.ds(c * LANES, LANES)] for c in range(chunks)]


def add_products(total, left, right):
    for a, b in zip(left, right):
        total = total + a * b
    return total


def zero_tile():
    return jnp.zeros((8, LANES), F32)


def inner_sweeps(refs, masks_ref, width_x, chunks):
    rims = (masks_ref[RIM], masks_ref[RIM + 1])
    for k in range(1, SWEEPS):
        for x in range(k, width_x - k):
            sweep_layer(refs[k - 1], refs[k], refs[0], x, k, rims, None, chunks)
    return [last_layer(refs[SWEEPS - 1], refs[0], x, chunks) for x in range(HALO, width_x - HALO)]


def outer_sweeps(refs, masks_ref, width_x, chunks):
    rims = (masks_ref[RIM], masks_ref[RIM + 1])
    for k in range(1, SWEEPS):
        for x in range(k - HALO, k):
            sweep_layer(refs[k - 1], refs[k], refs[0], x, k, rims, masks_ref[LEFT] if x < 0 else None, chunks)
            x = width_x - 1 - x
            keep = masks_ref[RIGHT] if x >= width_x else None
            sweep_layer(refs[k - 1], refs[k], refs[0], x, k, rims, keep, chunks)
    layers = (*range(HALO), *range(width_x - HALO, width_x))
    return [last_layer(refs[SWEEPS - 1], refs[0], x, chunks) for x in layers]


def half_block(shape):
    return jax.ShapeDtypeStruct((shape[0] - 2 * HALO,) + shape[1:], F32), jax.ShapeDtypeStruct(
        (2 * HALO,) + shape[1:], F32
    )


TILE = jax.ShapeDtypeStruct((8, LANES), F32)


def slope_inner_kernel(width_x, slope_ref, masks_ref, s_ref, one, two, three, raw_ref, square_ref):
    chunks = raw_ref.shape[2] // LANES
    s_ref[pl.ds(tall_row(0, 0, chunks), slope_ref.shape[0]), :] = slope_ref[...]
    total = zero_tile()
    for i, values in enumerate(inner_sweeps((s_ref, one, two, three), masks_ref, width_x, chunks)):
        store_layer(raw_ref, i, values)
        total = add_products(total, values, values)
    square_ref[...] = total


def make_slope_inner(s, masks, shape):
    wide = extended(shape)
    return pl.pallas_call(
        functools.partial(slope_inner_kernel, shape[0]),
        out_shape=(wide, wide, wide, wide, half_block(shape)[0], TILE),
        in_specs=[VMEM] * 2,
        out_specs=(VMEM,) * 6,
        compiler_params=params(8),
        cost_estimate=pl.CostEstimate(flops=15_000_000, bytes_accessed=8_000_000, transcendentals=0),
    )(s, masks)


def slope_outer_kernel(
    width_x, left_ref, right_ref, masks_ref, inner_square_ref, s_in, one_in, two_in, three_in,
    s_ref, one, two, three, raw_ref, square_ref,
):
    del s_in, one_in, two_in, three_in
    chunks = raw_ref.shape[2] // LANES
    read_faces(s_ref, left_ref, right_ref, masks_ref, width_x, chunks)
    total = inner_square_ref[...]
    for i, values in enumerate(outer_sweeps((s_ref, one, two, three), masks_ref, width_x, chunks)):
        store_layer(raw_ref, i, values)
        total = add_products(total, values, values)
    square_ref[...] = total


def make_slope_outer(left, right, masks, square, wide, shape):
    same = extended(shape)
    return pl.pallas_call(
        functools.partial(slope_outer_kernel, shape[0]),
        out_shape=(same, same, same, same, half_block(shape)[1], TILE),
        in_specs=[VMEM] * 8,
        out_specs=(VMEM,) * 6,
        input_output_aliases={4: 0, 5: 1, 6: 2, 7: 3},
        compiler_params=params(8),
        cost_estimate=pl.CostEstimate(flops=10_000_000, bytes_accessed=6_000_000, transcendentals=0),
    )(left, right, masks, square, *wide)[4:]


def source_inner_kernel(
    recv_ref, base_ref, slope_ref, masks_ref, slope_raw_ref, design_hbm, first_hbm, second_hbm, edges_ref,
    s_ref, one, two, three, raw_ref, sums_ref, design_ref, first_ref, second_ref, own, beside, sems,
):
    del edges_ref
    copies = start_all(((design_hbm, design_ref), (first_hbm, first_ref), (second_hbm, second_ref)), sems)
    width_x, width_y, width_z = design_ref.shape
    chunks = width_z // LANES
    scatter(recv_ref, own, beside, range(HALO, width_x - HALO, HALO), width_y * chunks)
    make_layers(range(HALO, width_x - HALO), s_ref, slope_ref, base_ref, own, beside, chunks)
    aa, ab = zero_tile(), zero_tile()
    for i, values in enumerate(inner_sweeps((s_ref, one, two, three), masks_ref, width_x, chunks)):
        store_layer(raw_ref, i, values)
        aa = add_products(aa, values, values)
        ab = add_products(ab, values, load_layer(slope_raw_ref, i, chunks))
    sums_ref[0] = aa
    sums_ref[1] = ab
    for copy in copies:
        copy.wait()


def make_source_inner(
    recv, base, slope, masks, slope_raw, design, first_moment, second_moment, edges
):
    block = jax.ShapeDtypeStruct(design.shape, F32)
    wide = extended(design.shape)
    scratch = pltpu.VMEM((design.size // LANES, LANES), F32)
    return pl.pallas_call(
        source_inner_kernel,
        out_shape=(wide,) * 4
        + (half_block(design.shape)[0], jax.ShapeDtypeStruct((2, 8, LANES), F32))
        + (block,) * 3,
        in_specs=[VMEM] * 5 + [HBM] * 3 + [VMEM],
        out_specs=(VMEM,) * 9,
        input_output_aliases={8: 0},
        scratch_shapes=[scratch] * 2 + [pltpu.SemaphoreType.DMA((3,))],
        compiler_params=params(8),
        cost_estimate=pl.CostEstimate(flops=40_000_000, bytes_accessed=16_000_000, transcendentals=0),
    )(
        recv, base, slope, masks, slope_raw,
        in_hbm(design), in_hbm(first_moment), in_hbm(second_moment), edges,
    )


def source_outer_kernel(
    width_x, left_ref, right_ref, masks_ref, slope_raw_ref, volume_ref, sums_ref, square_ref,
    s_in, one_in, two_in, three_in,
    s_ref, one, two, three, raw_ref, send_ref,
):
    del s_in, one_in, two_in, three_in
    chunks = raw_ref.shape[2] // LANES
    read_faces(s_ref, left_ref, right_ref, masks_ref, width_x, chunks)
    aa, ab = sums_ref[0], sums_ref[1]
    for i, values in enumerate(outer_sweeps((s_ref, one, two, three), masks_ref, width_x, chunks)):
        store_layer(raw_ref, i, values)
        aa = add_products(aa, values, values)
        ab = add_products(ab, values, load_layer(slope_raw_ref, i, chunks))
    lane = iota((1, LANES), 1)
    line = jnp.zeros((1, LANES), F32)
    for i, tile in enumerate((volume_ref[...], aa, ab, square_ref[...])):
        total = jnp.sum(tile, axis=0, keepdims=True)
        total = total + pltpu.roll(total, LANES // 2, 1)
        total = total + pltpu.roll(total, LANES // 4, 1)
        line = jnp.where(lane // (LANES // 4) == i, total, line)
    send_ref[...] = jnp.broadcast_to(line, send_ref.shape)


def make_source_outer(left, right, masks, slope_raw, volume, sums, square, wide, copies, shape):
    same = jax.ShapeDtypeStruct(wide[0].shape, F32)
    return pl.pallas_call(
        functools.partial(source_outer_kernel, shape[0]),
        out_shape=(same,) * 4 + (half_block(shape)[1], jax.ShapeDtypeStruct((copies, LANES), F32)),
        in_specs=[VMEM] * 11,
        out_specs=(VMEM,) * 6,
        input_output_aliases={7: 0, 8: 1, 9: 2, 10: 3},
        compiler_params=params(8),
    )(left, right, masks, slope_raw, volume, sums, square, *wide)[4:]


def adam_kernel(
    cells, sums_ref, masks_ref, inner_ref, outer_ref, slope_inner_ref, slope_outer_ref, design_ref, first_ref, second_ref,
    d_hbm, m_hbm, v_hbm, g_hbm, d_ref, m_ref, v_ref, g_ref, sems,
):
    width_x = design_ref.shape[0]
    line = jnp.sum(sums_ref[...], axis=0, keepdims=True)
    part = iota(line.shape, 1) // (LANES // 4)

    def picked(scale):
        return jnp.sum(line * scale, axis=1, keepdims=True)

    volume = picked(jnp.where(part == 0, 1.0, 0.0))
    shift = masks_ref[PENALTY, 0:1, 0:1] * (volume / cells / 0.4 - 1.25)
    total = picked(
        jnp.where(part == 1, 1.0, jnp.where(part == 2, 2.0 * shift, jnp.where(part == 3, shift * shift, 0.0)))
    )
    inverse = 1.0 / jnp.sqrt(jnp.maximum(total, 0.0) / cells + 1e-06)
    blocks = width_x // HALO
    copies = []
    for block in range(blocks):
        part = pl.ds(block * HALO, HALO)
        if block in (0, blocks - 1):
            raw, slope_raw, start = outer_ref, slope_outer_ref, 0 if block == 0 else HALO
        else:
            raw, slope_raw, start = inner_ref, slope_inner_ref, (block - 1) * HALO
        for i in range(HALO):
            x = block * HALO + i
            gradient = (raw[start + i] + shift * slope_raw[start + i]) * inverse
            new_first = 0.9 * first_ref[x] + 0.1 * gradient
            new_second = 0.999 * second_ref[x] + 0.001 * gradient * gradient
            first_hat = new_first * (0.05 / (1.0 - 0.9**ADAM_STEP))
            second_hat = new_second * (1.0 / (1.0 - 0.999**ADAM_STEP))
            d_ref[x] = jnp.clip(design_ref[x] - first_hat / (jnp.sqrt(second_hat) + 1e-08), 0.0, 1.0)
            m_ref[x] = new_first
            v_ref[x] = new_second
            g_ref[x] = gradient
        for i, (ref, hbm) in enumerate(((d_ref, d_hbm), (m_ref, m_hbm), (v_ref, v_hbm), (g_ref, g_hbm))):
            copy = pltpu.make_async_copy(ref.at[part], hbm.at[part], sems.at[block, i])
            copy.start()
            copies.append(copy)
    for copy in copies:
        copy.wait()


def adam(cells, sums, masks, parts, design, first_moment, second_moment):
    return pl.pallas_call(
        functools.partial(adam_kernel, cells),
        out_shape=(jax.ShapeDtypeStruct(design.shape, F32),) * 4,
        in_specs=[VMEM] * 9,
        out_specs=(HBM,) * 4,
        scratch_shapes=[pltpu.VMEM(design.shape, F32)] * 4 + [pltpu.SemaphoreType.DMA((4, 4))],
        compiler_params=params(8),
    )(sums, masks, *parts, design, first_moment, second_moment)


def shift(cells, axis, by):
    count = lax.axis_size(axis)
    return lax.ppermute(cells, axis, [(i, (i + by) % count) for i in range(count)])


def per_device(
    design,
    filtered,
    sensitivity,
    first_moment,
    second_moment,
    lagrange,
    trace_values,
    trace_anchor,
    trace_owner,
):
    width_x, width_y, depth = design.shape
    count_x, count_y = lax.axis_size("gx"), lax.axis_size("gy")
    cells = float(width_x * width_y * depth * count_x * count_y)
    rows = trace_values.shape[1]
    low, high, masks, packed, anchors = make_first(
        trace_values[0], trace_anchor, trace_owner.reshape(1, rows), lagrange.reshape(1, 2), filtered, sensitivity, count_y
    )
    below, above = shift(high, "gy", 1), shift(low, "gy", -1)
    sent = make_send(packed, anchors)
    received = lax.all_to_all(sent.reshape(count_y, SENT * LANES), "gy", 0, 0, tiled=True).reshape(sent.shape)

    slope, base, low, high, volume = make_slope(filtered, sensitivity, above, below, masks)
    left, right = shift(high, "gx", 1), shift(low, "gx", -1)
    shape = design.shape
    *wide, slope_inner, square = make_slope_inner(slope, masks, shape)
    slope_outer, square = make_slope_outer(left, right, masks, square, wide, shape)

    source, low, high = make_edges(received, base, slope, shape)
    left, right = shift(high, "gx", 1), shift(low, "gx", -1)
    *wide, inner, sums, design, first_moment, second_moment = make_source_inner(
        received, base, slope, masks, slope_inner, design, first_moment, second_moment, source
    )
    outer, sums = make_source_outer(
        left, right, masks, slope_outer, volume, sums, square, wide, count_x * count_y, shape
    )
    sums = lax.all_to_all(sums, ("gx", "gy"), 0, 0, tiled=True)
    parts = (inner, outer, slope_inner, slope_outer)
    return adam(cells, sums, masks, parts, design, first_moment, second_moment)


def solution(mesh):
    block = P("gx", "gy", None)
    return jax.shard_map(
        per_device,
        mesh=mesh,
        in_specs=(block, block, block, block, block, P(), block, P("gx", "gy"), block),
        out_specs=(block, block, block, block),
        check_vma=False,
    )
```

```python
import functools
import itertools

import jax
import jax.numpy as jnp
from jax import lax
from jax.experimental import pallas as pl
from jax.experimental.pallas import tpu as pltpu
from jax.sharding import PartitionSpec as P

SWEEPS = 4
ADAM_STEP = 10
CAP = 8
LANES = 128
HALO = 4
TALL = 16
GUARD = 8
FACE_ROWS = (8, 10, 12, 14)
FACE = sum(FACE_ROWS)
SENT = 3 * CAP + 1
GROUPS = LANES // CAP
LISTS = 5
LEFT, RIGHT, RIM, RIM_HALO, BASE, PENALTY = 0, 1, 2, 4, 5, 6
F32 = jnp.float32
BF16 = jnp.bfloat16
MIB = 1024 * 1024


def params(mib):
    return pltpu.CompilerParams(vmem_limit_bytes=mib * MIB)


VMEM = pl.BlockSpec(memory_space=pltpu.VMEM)
HBM = pl.BlockSpec(memory_space=pltpu.HBM)


def iota(shape, dim):
    return lax.broadcasted_iota(jnp.int32, shape, dim)


def in_hbm(array):
    return pltpu.with_memory_space_constraint(array, pltpu.HBM)


def start_all(pairs, sems):
    copies = [pltpu.make_async_copy(src, dst, sems.at[i]) for i, (src, dst) in enumerate(pairs)]
    for copy in copies:
        copy.start()
    return copies


def exact_parts(values):
    top = values.astype(BF16)
    rest = values - top.astype(F32)
    middle = rest.astype(BF16)
    last = (rest - middle.astype(F32)).astype(BF16)
    return jnp.concatenate([top, middle, last], axis=1)


def bucket_rows(values, anchor, owner, owners, chunks):
    rows = values.shape[0]
    place = (anchor // (8 * chunks)) * (8 * chunks) + (anchor % chunks) * 8 + (anchor // chunks) % 8
    down = iota((rows, rows), 0)
    across = iota((rows, rows), 1)
    owner_f = owner.astype(F32)
    owner_column = jnp.sum(
        jnp.where(down == across, jnp.broadcast_to(owner_f, (rows, rows)), 0.0), axis=1, keepdims=True
    )
    earlier = (owner_column == owner_f) & (down < across)
    rank = jnp.sum(jnp.where(earlier, 1.0, 0.0), axis=0, keepdims=True)
    slot = iota((owners * CAP, rows), 0)
    chosen = jnp.where((slot // CAP == owner) & ((slot % CAP).astype(F32) == rank), 1.0, 0.0).astype(BF16)
    added = jnp.dot(chosen, exact_parts(values), preferred_element_type=F32)
    packed = added[:, 0:LANES] + added[:, LANES : 2 * LANES] + added[:, 2 * LANES : 3 * LANES]
    named = jnp.where(iota((owners, rows), 0) == owner, 1.0, 0.0).astype(BF16)
    number = place + 1
    ranked = (iota((LANES, rows), 0) % CAP).astype(F32) == rank
    marked = jnp.concatenate(
        [jnp.where(ranked, t.astype(F32), 0.0).astype(BF16) for t in (number // 32, number % 32)], axis=0
    )
    found = lax.dot_general(named, marked, (((1,), (1,)), ((), ())), preferred_element_type=F32)
    return packed, 32.0 * found[:, 0:LANES] + found[:, LANES : 2 * LANES]


def first_kernel(
    values_hbm, anchor_hbm, owner_hbm, lagrange_hbm, filtered_hbm, sensitivity_hbm,
    low_ref, high_ref, masks_ref, packed_ref, anchors_ref,
    values_ref, anchor_ref, owner_ref, lagrange_ref, filtered_ref, sensitivity_ref, sems,
):
    copies = start_all(
        (
            (anchor_hbm, anchor_ref),
            (owner_hbm, owner_ref),
            (values_hbm, values_ref),
            (lagrange_hbm, lagrange_ref),
            (filtered_hbm, filtered_ref),
            (sensitivity_hbm, sensitivity_ref),
        ),
        sems,
    )
    width_x, width_y, width_z = filtered_ref.shape
    index_x, index_y = lax.axis_index("gx"), lax.axis_index("gy")
    one, zero = jnp.ones((8, LANES), F32), jnp.zeros((8, LANES), F32)
    upper = iota((8, LANES), 0) < 4
    before, after = jnp.where(index_y > 0, one, zero), jnp.where(index_y < lax.axis_size("gy") - 1, one, zero)
    masks_ref[LEFT] = jnp.where(index_x > 0, one, zero)
    masks_ref[RIGHT] = jnp.where(index_x < lax.axis_size("gx") - 1, one, zero)
    masks_ref[RIM] = jnp.where(upper, before, one)
    masks_ref[RIM + 1] = jnp.where(upper, one, after)
    masks_ref[RIM_HALO] = jnp.where(upper, after, before)
    for copy in copies[:4]:
        copy.wait()
    weight, penalty = lagrange_ref[0:1, 0:1], lagrange_ref[0:1, 1:2]
    masks_ref[BASE] = one * (weight + 0.25 * penalty)
    masks_ref[PENALTY] = one * penalty
    packed_ref[...], anchors_ref[...] = bucket_rows(
        values_ref[...], anchor_ref[...], owner_ref[...], anchors_ref.shape[0], width_z // LANES
    )
    half = iota((width_y, width_z), 0) < 4
    for f, ref in enumerate((filtered_ref, sensitivity_ref)):
        copies[4 + f].wait()
        for i in range(width_x // 2):
            even, odd = ref[2 * i], pltpu.roll(ref[2 * i + 1], 4, 0)
            low_ref[f, i] = jnp.where(half, even, odd)
            high_ref[f, i] = jnp.where(half, odd, even)


def make_first(values, anchor, owner, lagrange, filtered, sensitivity, owners):
    width_x, width_y, width_z = filtered.shape
    face = jax.ShapeDtypeStruct((2, width_x // 2, width_y, width_z), F32)
    return pl.pallas_call(
        first_kernel,
        out_shape=(
            face,
            face,
            jax.ShapeDtypeStruct((7, 8, LANES), F32),
            jax.ShapeDtypeStruct((owners * CAP, LANES), F32),
            jax.ShapeDtypeStruct((owners, LANES), F32),
        ),
        in_specs=[HBM] * 6,
        out_specs=(VMEM,) * 5,
        scratch_shapes=[
            pltpu.VMEM(values.shape, F32),
            pltpu.VMEM(anchor.shape, jnp.int32),
            pltpu.VMEM(owner.shape, jnp.int32),
            pltpu.VMEM(lagrange.shape, F32),
            pltpu.VMEM(filtered.shape, F32),
            pltpu.VMEM(filtered.shape, F32),
            pltpu.SemaphoreType.DMA((6,)),
        ],
        compiler_params=params(8),
    )(*[in_hbm(t) for t in (values, anchor, owner, lagrange, filtered, sensitivity)])


def send_kernel(packed_ref, anchors_ref, out_ref):
    owners = anchors_ref.shape[0]
    anchors = anchors_ref[...]
    lower = (anchors.astype(jnp.int32) - 1) % 8 < 4
    blank = jnp.zeros((1, LANES), F32)
    from_next = jnp.concatenate([jnp.where(lower, anchors, 0.0)[1:], blank], axis=0)
    from_last = jnp.concatenate([blank, jnp.where(lower, 0.0, anchors)[:-1]], axis=0)
    group = iota((owners, LANES), 1) // CAP
    me = lax.axis_index("gy")
    line = jnp.zeros((owners, LANES), F32)
    for i, part in enumerate((anchors, from_next, from_last)):
        line = jnp.where(group == (me + i * LISTS) % GROUPS, part, line)
    nothing = jnp.zeros((CAP, LANES), F32)
    for b in range(owners):
        for i, near in enumerate((b, b + 1, b - 1)):
            rows = packed_ref[near * CAP : (near + 1) * CAP, :] if 0 <= near < owners else nothing
            out_ref[b * SENT + i * CAP : b * SENT + (i + 1) * CAP, :] = rows
        out_ref[(b + 1) * SENT - 1 : (b + 1) * SENT, :] = line[b : b + 1]


def make_send(packed, anchors):
    return pl.pallas_call(
        send_kernel,
        out_shape=jax.ShapeDtypeStruct((anchors.shape[0] * SENT, LANES), F32),
        in_specs=[VMEM] * 2,
        out_specs=VMEM,
        compiler_params=params(8),
    )(packed, anchors)


def scatter(recv_ref, own, beside, layers, layer_rows):
    owners = recv_ref.shape[0] // SENT
    lines = recv_ref[pl.ds(SENT - 1, owners, stride=SENT), :]
    peer = iota((owners, LANES), 0)
    group = iota((owners, LANES), 1) // CAP

    def places(i):
        kept = jnp.where(group == (peer + i * LISTS) % GROUPS, lines, 0.0)
        sums = [jnp.sum(kept[g : g + GROUPS], axis=0, keepdims=True) for g in range(0, owners, GROUPS)]
        return [pltpu.roll(t, LANES - i * LISTS * CAP, 1) for t in sums] if i else sums

    def slots(i):
        return jnp.concatenate(
            [recv_ref[p * SENT + i * CAP : p * SENT + (i + 1) * CAP, :] for p in range(owners)], axis=0
        )

    for ref, lists in ((own, (0,)), (beside, (1, 2))):
        anchors = jnp.concatenate([t for i in lists for t in places(i)], axis=1)
        parts = jnp.concatenate([exact_parts(slots(i)) for i in lists], axis=0)
        for first in layers:
            start, step = first * layer_rows, HALO * layer_rows
            row = (iota((step, anchors.shape[1]), 0) + (start + 1)).astype(F32)
            hot = jnp.where(row == anchors, 1.0, 0.0).astype(BF16)
            added = jnp.dot(hot, parts, preferred_element_type=F32)
            ref[start : start + step, :] = (
                added[:, 0:LANES] + added[:, LANES : 2 * LANES] + added[:, 2 * LANES : 3 * LANES]
            )


def tall_tiles(half, inner, outer):
    return pltpu.roll(jnp.where(half, inner, outer), 4, 0), pltpu.roll(jnp.where(half, outer, inner), 4, 0)


def halo_tile(half, odd, low, high):
    return pltpu.roll(jnp.where(half, high, low), 4, 0) if odd else jnp.where(half, low, high)


def tall_row(x, c, chunks):
    return GUARD + ((x + HALO) * chunks + c) * TALL


def flat_row(x, c, chunks):
    return (x * chunks + c) * TALL


def face_rows(chunks):
    to = 0
    for d, count in zip(range(HALO, 0, -1), FACE_ROWS):
        skip = (TALL - count) // 2
        for c in range(chunks):
            for more in sorted({0, count - 8}):
                yield c, d, c // 2, (c % 2) * FACE + to + more, skip + more
        to += count


def fill_faces(s_ref, low_ref, high_ref, width_x, chunks, row_of):
    for c, d, page, line, skip in face_rows(chunks):
        for ref, x in ((low_ref, d - 1), (high_ref, width_x - d)):
            row = row_of(x, c, chunks) + skip
            ref[page, line : line + 8, :] = s_ref[pl.ds(row, 8), :]


def read_faces(s_ref, left_ref, right_ref, masks_ref, width_x, chunks):
    for c, d, page, line, skip in face_rows(chunks):
        for ref, x, keep in ((left_ref, -d, masks_ref[LEFT]), (right_ref, width_x - 1 + d, masks_ref[RIGHT])):
            row = tall_row(x, c, chunks) + skip
            s_ref[pl.ds(row, 8), :] = ref[page, line : line + 8, :] * keep


def extended(shape):
    width_x, width_y, width_z = shape
    return jax.ShapeDtypeStruct(((width_x + 2 * HALO) * (width_z // LANES) * TALL + 2 * GUARD, LANES), F32)


def flat(shape):
    return jax.ShapeDtypeStruct((shape[0] * (shape[2] // LANES) * TALL, LANES), F32)


def half_rows(rows):
    return jax.ShapeDtypeStruct((rows.shape[0] // 2, LANES), F32)


def face_shape(shape):
    return jax.ShapeDtypeStruct((shape[2] // LANES // 2, 2 * FACE, LANES), F32)


def slope_kernel(
    filtered_hbm, sensitivity_hbm, above_ref, below_ref, masks_ref,
    s_ref, edge_ref, inner_hbm, low_ref, high_ref, volume_ref, filtered_ref, sensitivity_ref, base_ref, sems,
):
    copies = start_all(((filtered_hbm, filtered_ref), (sensitivity_hbm, sensitivity_ref)), sems)
    width_x, width_y, width_z = filtered_ref.shape
    chunks = width_z // LANES
    edge = jnp.tanh(jnp.full((8, LANES), 4.0, F32))
    inverse = 1.0 / (edge + edge)
    eight = 8.0 * inverse
    half = iota((width_y, LANES), 0) < 4
    rim = masks_ref[RIM_HALO] * eight
    base = masks_ref[BASE]
    for copy in copies:
        copy.wait()

    def pair(i, total):
        for c, odd in itertools.product(range(chunks), range(2)):
            at, x = pl.ds(c * LANES, LANES), 2 * i + odd
            part = jnp.tanh(8.0 * (filtered_ref[x, :, at] - 0.5))
            total = total + (edge + part) * inverse
            side, sense = [halo_tile(half, odd, above_ref[f, i, :, at], below_ref[f, i, :, at]) for f in range(2)]
            side = jnp.tanh(8.0 * (side - 0.5))
            row = pl.multiple_of(flat_row(x, c, chunks), 8)
            for t, tile in enumerate(tall_tiles(half, (1.0 - part * part) * eight, (1.0 - side * side) * rim)):
                s_ref[pl.ds(row + 8 * t, 8), :] = tile
            for t, tile in enumerate(tall_tiles(half, sensitivity_ref[x, :, at], sense)):
                base_ref[pl.ds(row + 8 * t, 8), :] = tile + base
        return total

    volume_ref[...] = lax.fori_loop(0, width_x // 2, pair, jnp.zeros((8, LANES), F32))
    part = HALO * chunks * TALL
    copy = pltpu.make_async_copy(base_ref.at[pl.ds(part, 2 * part)], inner_hbm, sems.at[2])
    copy.start()
    edge_ref[0:part, :] = base_ref[0:part, :]
    edge_ref[part:, :] = base_ref[3 * part :, :]
    fill_faces(s_ref, low_ref, high_ref, width_x, chunks, flat_row)
    copy.wait()


def make_slope(filtered, sensitivity, above, below, masks):
    face = face_shape(filtered.shape)
    rows = flat(filtered.shape)
    part = half_rows(rows)
    block = pltpu.VMEM(filtered.shape, F32)
    return pl.pallas_call(
        slope_kernel,
        out_shape=(rows, part, part, face, face, jax.ShapeDtypeStruct((8, LANES), F32)),
        in_specs=[HBM] * 2 + [VMEM] * 3,
        out_specs=(VMEM, VMEM, HBM, VMEM, VMEM, VMEM),
        scratch_shapes=[block, block, pltpu.VMEM(rows.shape, F32), pltpu.SemaphoreType.DMA((3,))],
        compiler_params=params(8),
        cost_estimate=pl.CostEstimate(flops=4_000_000, bytes_accessed=4_000_000, transcendentals=300_000),
    )(in_hbm(filtered), in_hbm(sensitivity), above, below, masks)


def make_layers(layers, s_ref, slope_ref, base_ref, own, beside, chunks):
    half = iota((8, LANES), 0) < 4
    for (i, x), c in itertools.product(enumerate(layers), range(chunks)):
        line = pl.ds((x * chunks + c) * 8, 8)
        for t, tile in enumerate(tall_tiles(half, own[line, :], beside[line, :])):
            slope = slope_ref[pl.ds(flat_row(x, c, chunks) + 8 * t, 8), :]
            base = base_ref[pl.ds(flat_row(i, c, chunks) + 8 * t, 8), :]
            s_ref[pl.ds(tall_row(x, c, chunks) + 8 * t, 8), :] = slope * (base + tile)


def edge_kernel(width_x, recv_ref, base_ref, slope_ref, s_ref, low_ref, high_ref, own, beside):
    layer_rows = own.shape[0] // width_x
    chunks = layer_rows // 8
    scatter(recv_ref, own, beside, (0, width_x - HALO), layer_rows)
    layers = (*range(HALO), *range(width_x - HALO, width_x))
    make_layers(layers, s_ref, slope_ref, base_ref, own, beside, chunks)
    fill_faces(s_ref, low_ref, high_ref, width_x, chunks, tall_row)


def make_edges(recv, base, slope, shape):
    width_x, width_y, width_z = shape
    face = face_shape(shape)
    scratch = pltpu.VMEM((width_x * width_y * width_z // LANES, LANES), F32)
    return pl.pallas_call(
        functools.partial(edge_kernel, width_x),
        out_shape=(extended(shape), face, face),
        in_specs=[VMEM] * 3,
        out_specs=(VMEM,) * 3,
        scratch_shapes=[scratch] * 2,
        compiler_params=params(8),
    )(recv, base, slope)


def weight_of(k):
    return (25.0 / 4.0) ** k / 25.0


def sweep(ref, source, base, k, chunks):
    layer = chunks * TALL
    lane = iota((8, LANES), 1)
    own = [ref[pl.ds(base + c * TALL, 8), :] for c in range(chunks)]
    up = [pltpu.roll(t, LANES - 1, 1) for t in own]
    down = [pltpu.roll(t, 1, 1) for t in own]
    zero = jnp.zeros((8, LANES), F32)
    results = []
    for c in range(chunks):
        at = base + c * TALL
        total = jnp.where(lane == LANES - 1, up[c + 1] if c + 1 < chunks else zero, up[c])
        total = total + jnp.where(lane == 0, down[c - 1] if c else zero, down[c])
        total = total + (ref[pl.ds(at - 1, 8), :] + ref[pl.ds(at + 1, 8), :])
        total = total + (ref[pl.ds(at - layer, 8), :] + ref[pl.ds(at + layer, 8), :])
        results.append(total + weight_of(k) * source[pl.ds(at, 8), :])
    return results


def sweep_layer(old, new, source, x, k, rims, keep, chunks):
    for tile in range(2):
        mask = rims[tile] if keep is None else rims[tile] * keep
        base = tall_row(x, 0, chunks) + 8 * tile
        for c, value in enumerate(sweep(old, source, base, k, chunks)):
            new[pl.ds(base + c * TALL, 8), :] = value * mask


def last_layer(old, source, x, chunks):
    scale = (4.0 / 25.0) ** SWEEPS
    return [scale * t for t in sweep(old, source, tall_row(x, 0, chunks) + HALO, SWEEPS, chunks)]


def store_layer(ref, x, values):
    for c, value in enumerate(values):
        ref[x, :, pl.ds(c * LANES, LANES)] = value


def load_layer(ref, x, chunks):
    return [ref[x, :, pl.ds(c * LANES, LANES)] for c in range(chunks)]


def add_products(total, left, right):
    for a, b in zip(left, right):
        total = total + a * b
    return total


def zero_tile():
    return jnp.zeros((8, LANES), F32)


def inner_sweeps(refs, masks_ref, width_x, chunks):
    rims = (masks_ref[RIM], masks_ref[RIM + 1])
    for k in range(1, SWEEPS):
        for x in range(k, width_x - k):
            sweep_layer(refs[k - 1], refs[k], refs[0], x, k, rims, None, chunks)
    return [last_layer(refs[SWEEPS - 1], refs[0], x, chunks) for x in range(HALO, width_x - HALO)]


def outer_sweeps(refs, masks_ref, width_x, chunks):
    rims = (masks_ref[RIM], masks_ref[RIM + 1])
    for k in range(1, SWEEPS):
        for x in range(k - HALO, k):
            sweep_layer(refs[k - 1], refs[k], refs[0], x, k, rims, masks_ref[LEFT] if x < 0 else None, chunks)
            x = width_x - 1 - x
            keep = masks_ref[RIGHT] if x >= width_x else None
            sweep_layer(refs[k - 1], refs[k], refs[0], x, k, rims, keep, chunks)
    layers = (*range(HALO), *range(width_x - HALO, width_x))
    return [last_layer(refs[SWEEPS - 1], refs[0], x, chunks) for x in layers]


def half_block(shape):
    return jax.ShapeDtypeStruct((shape[0] - 2 * HALO,) + shape[1:], F32), jax.ShapeDtypeStruct(
        (2 * HALO,) + shape[1:], F32
    )


TILE = jax.ShapeDtypeStruct((8, LANES), F32)


def slope_inner_kernel(
    width_x, slope_ref, masks_ref, base_hbm, design_hbm, s_ref, one, two, three, raw_ref, square_ref, base_ref, design_ref, sems
):
    copies = start_all(((base_hbm, base_ref), (design_hbm, design_ref)), sems)
    chunks = raw_ref.shape[2] // LANES
    s_ref[pl.ds(tall_row(0, 0, chunks), slope_ref.shape[0]), :] = slope_ref[...]
    total = zero_tile()
    for i, values in enumerate(inner_sweeps((s_ref, one, two, three), masks_ref, width_x, chunks)):
        store_layer(raw_ref, i, values)
        total = add_products(total, values, values)
    square_ref[...] = total
    for copy in copies:
        copy.wait()


def make_slope_inner(s, masks, base, design):
    shape = design.shape
    wide = extended(shape)
    return pl.pallas_call(
        functools.partial(slope_inner_kernel, shape[0]),
        out_shape=(wide, wide, wide, wide, half_block(shape)[0], TILE)
        + (jax.ShapeDtypeStruct(base.shape, F32), jax.ShapeDtypeStruct(shape, F32)),
        in_specs=[VMEM] * 2 + [HBM] * 2,
        out_specs=(VMEM,) * 8,
        scratch_shapes=[pltpu.SemaphoreType.DMA((2,))],
        compiler_params=params(8),
        cost_estimate=pl.CostEstimate(flops=15_000_000, bytes_accessed=8_000_000, transcendentals=0),
    )(s, masks, in_hbm(base), in_hbm(design))


def slope_outer_kernel(
    width_x, left_ref, right_ref, masks_ref, inner_square_ref, s_in, one_in, two_in, three_in, second_hbm,
    s_ref, one, two, three, raw_ref, square_ref, second_ref, sems,
):
    del s_in, one_in, two_in, three_in
    (copy,) = start_all(((second_hbm, second_ref),), sems)
    chunks = raw_ref.shape[2] // LANES
    read_faces(s_ref, left_ref, right_ref, masks_ref, width_x, chunks)
    total = inner_square_ref[...]
    for i, values in enumerate(outer_sweeps((s_ref, one, two, three), masks_ref, width_x, chunks)):
        store_layer(raw_ref, i, values)
        total = add_products(total, values, values)
    square_ref[...] = total
    copy.wait()


def make_slope_outer(left, right, masks, square, wide, second_moment):
    shape = second_moment.shape
    same = extended(shape)
    return pl.pallas_call(
        functools.partial(slope_outer_kernel, shape[0]),
        out_shape=(same, same, same, same, half_block(shape)[1], TILE, jax.ShapeDtypeStruct(shape, F32)),
        in_specs=[VMEM] * 8 + [HBM],
        out_specs=(VMEM,) * 7,
        scratch_shapes=[pltpu.SemaphoreType.DMA((1,))],
        input_output_aliases={4: 0, 5: 1, 6: 2, 7: 3},
        compiler_params=params(8),
        cost_estimate=pl.CostEstimate(flops=10_000_000, bytes_accessed=6_000_000, transcendentals=0),
    )(left, right, masks, square, *wide, in_hbm(second_moment))[4:]


def source_inner_kernel(
    recv_ref, base_ref, slope_ref, masks_ref, slope_raw_ref, first_hbm, edges_ref,
    s_ref, one, two, three, raw_ref, sums_ref, first_ref, own, beside, sems,
):
    del edges_ref
    (copy,) = start_all(((first_hbm, first_ref),), sems)
    width_x, width_y, width_z = first_ref.shape
    chunks = width_z // LANES
    scatter(recv_ref, own, beside, range(HALO, width_x - HALO, HALO), width_y * chunks)
    make_layers(range(HALO, width_x - HALO), s_ref, slope_ref, base_ref, own, beside, chunks)
    aa, ab = zero_tile(), zero_tile()
    for i, values in enumerate(inner_sweeps((s_ref, one, two, three), masks_ref, width_x, chunks)):
        store_layer(raw_ref, i, values)
        aa = add_products(aa, values, values)
        ab = add_products(ab, values, load_layer(slope_raw_ref, i, chunks))
    sums_ref[0] = aa
    sums_ref[1] = ab
    copy.wait()


def make_source_inner(recv, base, slope, masks, slope_raw, first_moment, edges):
    shape = first_moment.shape
    wide = extended(shape)
    scratch = pltpu.VMEM((first_moment.size // LANES, LANES), F32)
    return pl.pallas_call(
        source_inner_kernel,
        out_shape=(wide,) * 4
        + (half_block(shape)[0], jax.ShapeDtypeStruct((2, 8, LANES), F32), jax.ShapeDtypeStruct(shape, F32)),
        in_specs=[VMEM] * 5 + [HBM] + [VMEM],
        out_specs=(VMEM,) * 7,
        input_output_aliases={6: 0},
        scratch_shapes=[scratch] * 2 + [pltpu.SemaphoreType.DMA((1,))],
        compiler_params=params(8),
        cost_estimate=pl.CostEstimate(flops=40_000_000, bytes_accessed=16_000_000, transcendentals=0),
    )(recv, base, slope, masks, slope_raw, in_hbm(first_moment), edges)


def source_outer_kernel(
    width_x, left_ref, right_ref, masks_ref, slope_raw_ref, volume_ref, sums_ref, square_ref,
    s_in, one_in, two_in, three_in,
    s_ref, one, two, three, raw_ref, send_ref,
):
    del s_in, one_in, two_in, three_in
    chunks = raw_ref.shape[2] // LANES
    read_faces(s_ref, left_ref, right_ref, masks_ref, width_x, chunks)
    aa, ab = sums_ref[0], sums_ref[1]
    for i, values in enumerate(outer_sweeps((s_ref, one, two, three), masks_ref, width_x, chunks)):
        store_layer(raw_ref, i, values)
        aa = add_products(aa, values, values)
        ab = add_products(ab, values, load_layer(slope_raw_ref, i, chunks))
    lane = iota((1, LANES), 1)
    line = jnp.zeros((1, LANES), F32)
    for i, tile in enumerate((volume_ref[...], aa, ab, square_ref[...])):
        total = jnp.sum(tile, axis=0, keepdims=True)
        total = total + pltpu.roll(total, LANES // 2, 1)
        total = total + pltpu.roll(total, LANES // 4, 1)
        line = jnp.where(lane // (LANES // 4) == i, total, line)
    send_ref[...] = jnp.broadcast_to(line, send_ref.shape)


def make_source_outer(left, right, masks, slope_raw, volume, sums, square, wide, copies, shape):
    same = jax.ShapeDtypeStruct(wide[0].shape, F32)
    return pl.pallas_call(
        functools.partial(source_outer_kernel, shape[0]),
        out_shape=(same,) * 4 + (half_block(shape)[1], jax.ShapeDtypeStruct((copies, LANES), F32)),
        in_specs=[VMEM] * 11,
        out_specs=(VMEM,) * 6,
        input_output_aliases={7: 0, 8: 1, 9: 2, 10: 3},
        compiler_params=params(8),
    )(left, right, masks, slope_raw, volume, sums, square, *wide)[4:]


def adam_kernel(
    cells, sums_ref, masks_ref, inner_ref, outer_ref, slope_inner_ref, slope_outer_ref, design_ref, first_ref, second_ref,
    d_hbm, m_hbm, v_hbm, g_hbm, d_ref, m_ref, v_ref, g_ref, sems,
):
    width_x = design_ref.shape[0]
    line = jnp.sum(sums_ref[...], axis=0, keepdims=True)
    part = iota(line.shape, 1) // (LANES // 4)

    def picked(scale):
        return jnp.sum(line * scale, axis=1, keepdims=True)

    volume = picked(jnp.where(part == 0, 1.0, 0.0))
    shift = masks_ref[PENALTY, 0:1, 0:1] * (volume / cells / 0.4 - 1.25)
    total = picked(
        jnp.where(part == 1, 1.0, jnp.where(part == 2, 2.0 * shift, jnp.where(part == 3, shift * shift, 0.0)))
    )
    inverse = 1.0 / jnp.sqrt(jnp.maximum(total, 0.0) / cells + 1e-06)
    blocks = width_x // HALO
    copies = []
    for block in range(blocks):
        part = pl.ds(block * HALO, HALO)
        if block in (0, blocks - 1):
            raw, slope_raw, start = outer_ref, slope_outer_ref, 0 if block == 0 else HALO
        else:
            raw, slope_raw, start = inner_ref, slope_inner_ref, (block - 1) * HALO
        for i in range(HALO):
            x = block * HALO + i
            gradient = (raw[start + i] + shift * slope_raw[start + i]) * inverse
            new_first = 0.9 * first_ref[x] + 0.1 * gradient
            new_second = 0.999 * second_ref[x] + 0.001 * gradient * gradient
            first_hat = new_first * (0.05 / (1.0 - 0.9**ADAM_STEP))
            second_hat = new_second * (1.0 / (1.0 - 0.999**ADAM_STEP))
            d_ref[x] = jnp.clip(design_ref[x] - first_hat / (jnp.sqrt(second_hat) + 1e-08), 0.0, 1.0)
            m_ref[x] = new_first
            v_ref[x] = new_second
            g_ref[x] = gradient
        for i, (ref, hbm) in enumerate(((d_ref, d_hbm), (m_ref, m_hbm), (v_ref, v_hbm), (g_ref, g_hbm))):
            copy = pltpu.make_async_copy(ref.at[part], hbm.at[part], sems.at[block, i])
            copy.start()
            copies.append(copy)
    for copy in copies:
        copy.wait()


def adam(cells, sums, masks, parts, design, first_moment, second_moment):
    return pl.pallas_call(
        functools.partial(adam_kernel, cells),
        out_shape=(jax.ShapeDtypeStruct(design.shape, F32),) * 4,
        in_specs=[VMEM] * 9,
        out_specs=(HBM,) * 4,
        scratch_shapes=[pltpu.VMEM(design.shape, F32)] * 4 + [pltpu.SemaphoreType.DMA((4, 4))],
        compiler_params=params(8),
    )(sums, masks, *parts, design, first_moment, second_moment)


def shift(cells, axis, by):
    count = lax.axis_size(axis)
    return lax.ppermute(cells, axis, [(i, (i + by) % count) for i in range(count)])


def per_device(
    design,
    filtered,
    sensitivity,
    first_moment,
    second_moment,
    lagrange,
    trace_values,
    trace_anchor,
    trace_owner,
):
    width_x, width_y, depth = design.shape
    count_x, count_y = lax.axis_size("gx"), lax.axis_size("gy")
    cells = float(width_x * width_y * depth * count_x * count_y)
    rows = trace_values.shape[1]
    low, high, masks, packed, anchors = make_first(
        trace_values[0], trace_anchor, trace_owner.reshape(1, rows), lagrange.reshape(1, 2), filtered, sensitivity, count_y
    )
    below, above = shift(high, "gy", 1), shift(low, "gy", -1)
    sent = make_send(packed, anchors)
    received = lax.all_to_all(sent.reshape(count_y, SENT * LANES), "gy", 0, 0, tiled=True).reshape(sent.shape)

    slope, base_edges, base, low, high, volume = make_slope(filtered, sensitivity, above, below, masks)
    left, right = shift(high, "gx", 1), shift(low, "gx", -1)
    shape = design.shape
    *wide, slope_inner, square, base, design = make_slope_inner(slope, masks, base, design)
    slope_outer, square, second_moment = make_slope_outer(left, right, masks, square, wide, second_moment)

    source, low, high = make_edges(received, base_edges, slope, shape)
    left, right = shift(high, "gx", 1), shift(low, "gx", -1)
    *wide, inner, sums, first_moment = make_source_inner(
        received, base, slope, masks, slope_inner, first_moment, source
    )
    outer, sums = make_source_outer(
        left, right, masks, slope_outer, volume, sums, square, wide, count_x * count_y, shape
    )
    sums = lax.all_to_all(sums, ("gx", "gy"), 0, 0, tiled=True)
    parts = (inner, outer, slope_inner, slope_outer)
    return adam(cells, sums, masks, parts, design, first_moment, second_moment)


def solution(mesh):
    block = P("gx", "gy", None)
    return jax.shard_map(
        per_device,
        mesh=mesh,
        in_specs=(block, block, block, block, block, P(), block, P("gx", "gy"), block),
        out_specs=(block, block, block, block),
        check_vma=False,
    )
```

```python
import functools
import itertools

import jax
import jax.numpy as jnp
from jax import lax
from jax.experimental import pallas as pl
from jax.experimental.pallas import tpu as pltpu
from jax.sharding import PartitionSpec as P

SWEEPS = 4
ADAM_STEP = 10
CAP = 8
LANES = 128
HALO = 4
TALL = 16
GUARD = 8
FACE_ROWS = (8, 10, 12, 14)
FACE = sum(FACE_ROWS)
SENT = 3 * CAP + 1
GROUPS = LANES // CAP
LISTS = 5
LEFT, RIGHT, RIM, RIM_HALO, BASE, PENALTY = 0, 1, 2, 4, 5, 6
F32 = jnp.float32
BF16 = jnp.bfloat16
MIB = 1024 * 1024


def params(mib):
    return pltpu.CompilerParams(vmem_limit_bytes=mib * MIB)


VMEM = pl.BlockSpec(memory_space=pltpu.VMEM)
HBM = pl.BlockSpec(memory_space=pltpu.HBM)


def iota(shape, dim):
    return lax.broadcasted_iota(jnp.int32, shape, dim)


def in_hbm(array):
    return pltpu.with_memory_space_constraint(array, pltpu.HBM)


def start_all(pairs, sems):
    copies = [pltpu.make_async_copy(src, dst, sems.at[i]) for i, (src, dst) in enumerate(pairs)]
    for copy in copies:
        copy.start()
    return copies


def exact_parts(values):
    top = values.astype(BF16)
    rest = values - top.astype(F32)
    middle = rest.astype(BF16)
    last = (rest - middle.astype(F32)).astype(BF16)
    return jnp.concatenate([top, middle, last], axis=1)


def bucket_rows(values, anchor, owner, owners, chunks):
    rows = values.shape[0]
    place = (anchor // (8 * chunks)) * (8 * chunks) + (anchor % chunks) * 8 + (anchor // chunks) % 8
    down = iota((rows, rows), 0)
    across = iota((rows, rows), 1)
    owner_f = owner.astype(F32)
    owner_column = jnp.sum(
        jnp.where(down == across, jnp.broadcast_to(owner_f, (rows, rows)), 0.0), axis=1, keepdims=True
    )
    earlier = (owner_column == owner_f) & (down < across)
    rank = jnp.sum(jnp.where(earlier, 1.0, 0.0), axis=0, keepdims=True)
    slot = iota((owners * CAP, rows), 0)
    chosen = jnp.where((slot // CAP == owner) & ((slot % CAP).astype(F32) == rank), 1.0, 0.0).astype(BF16)
    added = jnp.dot(chosen, exact_parts(values), preferred_element_type=F32)
    packed = added[:, 0:LANES] + added[:, LANES : 2 * LANES] + added[:, 2 * LANES : 3 * LANES]
    named = jnp.where(iota((owners, rows), 0) == owner, 1.0, 0.0).astype(BF16)
    number = place + 1
    ranked = (iota((LANES, rows), 0) % CAP).astype(F32) == rank
    marked = jnp.concatenate(
        [jnp.where(ranked, t.astype(F32), 0.0).astype(BF16) for t in (number // 32, number % 32)], axis=0
    )
    found = lax.dot_general(named, marked, (((1,), (1,)), ((), ())), preferred_element_type=F32)
    return packed, 32.0 * found[:, 0:LANES] + found[:, LANES : 2 * LANES]


def first_kernel(
    values_hbm, anchor_hbm, owner_hbm, lagrange_hbm, filtered_hbm, sensitivity_hbm,
    low_ref, high_ref, masks_ref, packed_ref, anchors_ref,
    values_ref, anchor_ref, owner_ref, lagrange_ref, filtered_ref, sensitivity_ref, sems,
):
    copies = start_all(
        (
            (anchor_hbm, anchor_ref),
            (owner_hbm, owner_ref),
            (values_hbm, values_ref),
            (lagrange_hbm, lagrange_ref),
            (filtered_hbm, filtered_ref),
            (sensitivity_hbm, sensitivity_ref),
        ),
        sems,
    )
    width_x, width_y, width_z = filtered_ref.shape
    index_x, index_y = lax.axis_index("gx"), lax.axis_index("gy")
    one, zero = jnp.ones((8, LANES), F32), jnp.zeros((8, LANES), F32)
    upper = iota((8, LANES), 0) < 4
    before, after = jnp.where(index_y > 0, one, zero), jnp.where(index_y < lax.axis_size("gy") - 1, one, zero)
    masks_ref[LEFT] = jnp.where(index_x > 0, one, zero)
    masks_ref[RIGHT] = jnp.where(index_x < lax.axis_size("gx") - 1, one, zero)
    masks_ref[RIM] = jnp.where(upper, before, one)
    masks_ref[RIM + 1] = jnp.where(upper, one, after)
    masks_ref[RIM_HALO] = jnp.where(upper, after, before)
    for copy in copies[:4]:
        copy.wait()
    weight, penalty = lagrange_ref[0:1, 0:1], lagrange_ref[0:1, 1:2]
    masks_ref[BASE] = one * (weight + 0.25 * penalty)
    masks_ref[PENALTY] = one * penalty
    packed_ref[...], anchors_ref[...] = bucket_rows(
        values_ref[...], anchor_ref[...], owner_ref[...], anchors_ref.shape[0], width_z // LANES
    )
    half = iota((width_y, width_z), 0) < 4
    for f, ref in enumerate((filtered_ref, sensitivity_ref)):
        copies[4 + f].wait()
        for i in range(width_x // 2):
            even, odd = ref[2 * i], pltpu.roll(ref[2 * i + 1], 4, 0)
            low_ref[f, i] = jnp.where(half, even, odd)
            high_ref[f, i] = jnp.where(half, odd, even)


def make_first(values, anchor, owner, lagrange, filtered, sensitivity, owners):
    width_x, width_y, width_z = filtered.shape
    face = jax.ShapeDtypeStruct((2, width_x // 2, width_y, width_z), F32)
    return pl.pallas_call(
        first_kernel,
        out_shape=(
            face,
            face,
            jax.ShapeDtypeStruct((7, 8, LANES), F32),
            jax.ShapeDtypeStruct((owners * CAP, LANES), F32),
            jax.ShapeDtypeStruct((owners, LANES), F32),
        ),
        in_specs=[HBM] * 6,
        out_specs=(VMEM,) * 5,
        scratch_shapes=[
            pltpu.VMEM(values.shape, F32),
            pltpu.VMEM(anchor.shape, jnp.int32),
            pltpu.VMEM(owner.shape, jnp.int32),
            pltpu.VMEM(lagrange.shape, F32),
            pltpu.VMEM(filtered.shape, F32),
            pltpu.VMEM(filtered.shape, F32),
            pltpu.SemaphoreType.DMA((6,)),
        ],
        compiler_params=params(8),
    )(*[in_hbm(t) for t in (values, anchor, owner, lagrange, filtered, sensitivity)])


def send_kernel(packed_ref, anchors_ref, out_ref):
    owners = anchors_ref.shape[0]
    anchors = anchors_ref[...]
    lower = (anchors.astype(jnp.int32) - 1) % 8 < 4
    blank = jnp.zeros((1, LANES), F32)
    from_next = jnp.concatenate([jnp.where(lower, anchors, 0.0)[1:], blank], axis=0)
    from_last = jnp.concatenate([blank, jnp.where(lower, 0.0, anchors)[:-1]], axis=0)
    group = iota((owners, LANES), 1) // CAP
    me = lax.axis_index("gy")
    line = jnp.zeros((owners, LANES), F32)
    for i, part in enumerate((anchors, from_next, from_last)):
        line = jnp.where(group == (me + i * LISTS) % GROUPS, part, line)
    nothing = jnp.zeros((CAP, LANES), F32)
    for b in range(owners):
        for i, near in enumerate((b, b + 1, b - 1)):
            rows = packed_ref[near * CAP : (near + 1) * CAP, :] if 0 <= near < owners else nothing
            out_ref[b * SENT + i * CAP : b * SENT + (i + 1) * CAP, :] = rows
        out_ref[(b + 1) * SENT - 1 : (b + 1) * SENT, :] = line[b : b + 1]


def make_send(packed, anchors):
    return pl.pallas_call(
        send_kernel,
        out_shape=jax.ShapeDtypeStruct((anchors.shape[0] * SENT, LANES), F32),
        in_specs=[VMEM] * 2,
        out_specs=VMEM,
        compiler_params=params(8),
    )(packed, anchors)


def scatter(recv_ref, own, beside, layers, layer_rows):
    owners = recv_ref.shape[0] // SENT
    lines = recv_ref[pl.ds(SENT - 1, owners, stride=SENT), :]
    peer = iota((owners, LANES), 0)
    group = iota((owners, LANES), 1) // CAP

    def places(i):
        kept = jnp.where(group == (peer + i * LISTS) % GROUPS, lines, 0.0)
        sums = [jnp.sum(kept[g : g + GROUPS], axis=0, keepdims=True) for g in range(0, owners, GROUPS)]
        return [pltpu.roll(t, LANES - i * LISTS * CAP, 1) for t in sums] if i else sums

    def slots(i):
        return jnp.concatenate(
            [recv_ref[p * SENT + i * CAP : p * SENT + (i + 1) * CAP, :] for p in range(owners)], axis=0
        )

    for ref, lists in ((own, (0,)), (beside, (1, 2))):
        anchors = jnp.concatenate([t for i in lists for t in places(i)], axis=1)
        parts = jnp.concatenate([exact_parts(slots(i)) for i in lists], axis=0)
        for first in layers:
            start, step = first * layer_rows, HALO * layer_rows
            row = (iota((step, anchors.shape[1]), 0) + (start + 1)).astype(F32)
            hot = jnp.where(row == anchors, 1.0, 0.0).astype(BF16)
            added = jnp.dot(hot, parts, preferred_element_type=F32)
            ref[start : start + step, :] = (
                added[:, 0:LANES] + added[:, LANES : 2 * LANES] + added[:, 2 * LANES : 3 * LANES]
            )


def tall_tiles(half, inner, outer):
    return pltpu.roll(jnp.where(half, inner, outer), 4, 0), pltpu.roll(jnp.where(half, outer, inner), 4, 0)


def halo_tile(half, odd, low, high):
    return pltpu.roll(jnp.where(half, high, low), 4, 0) if odd else jnp.where(half, low, high)


def tall_row(x, c, chunks):
    return GUARD + ((x + HALO) * chunks + c) * TALL


def flat_row(x, c, chunks):
    return (x * chunks + c) * TALL


def face_rows(chunks):
    to = 0
    for d, count in zip(range(HALO, 0, -1), FACE_ROWS):
        skip = (TALL - count) // 2
        for c in range(chunks):
            for more in sorted({0, count - 8}):
                yield c, d, c // 2, (c % 2) * FACE + to + more, skip + more
        to += count


def fill_faces(s_ref, low_ref, high_ref, width_x, chunks, row_of):
    for c, d, page, line, skip in face_rows(chunks):
        for ref, x in ((low_ref, d - 1), (high_ref, width_x - d)):
            row = row_of(x, c, chunks) + skip
            ref[page, line : line + 8, :] = s_ref[pl.ds(row, 8), :]


def read_faces(s_ref, left_ref, right_ref, masks_ref, width_x, chunks):
    for c, d, page, line, skip in face_rows(chunks):
        for ref, x, keep in ((left_ref, -d, masks_ref[LEFT]), (right_ref, width_x - 1 + d, masks_ref[RIGHT])):
            row = tall_row(x, c, chunks) + skip
            s_ref[pl.ds(row, 8), :] = ref[page, line : line + 8, :] * keep


def extended(shape):
    width_x, width_y, width_z = shape
    return jax.ShapeDtypeStruct(((width_x + 2 * HALO) * (width_z // LANES) * TALL + 2 * GUARD, LANES), F32)


def flat(shape):
    return jax.ShapeDtypeStruct((shape[0] * (shape[2] // LANES) * TALL, LANES), F32)


def half_rows(rows):
    return jax.ShapeDtypeStruct((rows.shape[0] // 2, LANES), F32)


def face_shape(shape):
    return jax.ShapeDtypeStruct((shape[2] // LANES // 2, 2 * FACE, LANES), F32)


def slope_kernel(
    filtered_hbm, sensitivity_hbm, above_ref, below_ref, masks_ref,
    s_ref, edge_ref, inner_hbm, low_ref, high_ref, volume_ref, filtered_ref, sensitivity_ref, base_ref, sems,
):
    copies = start_all(((filtered_hbm, filtered_ref), (sensitivity_hbm, sensitivity_ref)), sems)
    width_x, width_y, width_z = filtered_ref.shape
    chunks = width_z // LANES
    edge = jnp.tanh(jnp.full((8, LANES), 4.0, F32))
    inverse = 1.0 / (edge + edge)
    eight = 8.0 * inverse
    half = iota((width_y, LANES), 0) < 4
    rim = masks_ref[RIM_HALO] * eight
    base = masks_ref[BASE]
    for copy in copies:
        copy.wait()

    def pair(i, total):
        for c, odd in itertools.product(range(chunks), range(2)):
            at, x = pl.ds(c * LANES, LANES), 2 * i + odd
            part = jnp.tanh(8.0 * (filtered_ref[x, :, at] - 0.5))
            total = total + (edge + part) * inverse
            side, sense = [halo_tile(half, odd, above_ref[f, i, :, at], below_ref[f, i, :, at]) for f in range(2)]
            side = jnp.tanh(8.0 * (side - 0.5))
            row = pl.multiple_of(flat_row(x, c, chunks), 8)
            for t, tile in enumerate(tall_tiles(half, (1.0 - part * part) * eight, (1.0 - side * side) * rim)):
                s_ref[pl.ds(row + 8 * t, 8), :] = tile
            for t, tile in enumerate(tall_tiles(half, sensitivity_ref[x, :, at], sense)):
                base_ref[pl.ds(row + 8 * t, 8), :] = tile + base
        return total

    volume_ref[...] = lax.fori_loop(0, width_x // 2, pair, jnp.zeros((8, LANES), F32))
    part = HALO * chunks * TALL
    copy = pltpu.make_async_copy(base_ref.at[pl.ds(part, 2 * part)], inner_hbm, sems.at[2])
    copy.start()
    edge_ref[0:part, :] = base_ref[0:part, :]
    edge_ref[part:, :] = base_ref[3 * part :, :]
    fill_faces(s_ref, low_ref, high_ref, width_x, chunks, flat_row)
    copy.wait()


def make_slope(filtered, sensitivity, above, below, masks):
    face = face_shape(filtered.shape)
    rows = flat(filtered.shape)
    part = half_rows(rows)
    block = pltpu.VMEM(filtered.shape, F32)
    return pl.pallas_call(
        slope_kernel,
        out_shape=(rows, part, part, face, face, jax.ShapeDtypeStruct((8, LANES), F32)),
        in_specs=[HBM] * 2 + [VMEM] * 3,
        out_specs=(VMEM, VMEM, HBM, VMEM, VMEM, VMEM),
        scratch_shapes=[block, block, pltpu.VMEM(rows.shape, F32), pltpu.SemaphoreType.DMA((3,))],
        compiler_params=params(8),
        cost_estimate=pl.CostEstimate(flops=4_000_000, bytes_accessed=4_000_000, transcendentals=300_000),
    )(in_hbm(filtered), in_hbm(sensitivity), above, below, masks)


def make_layers(layers, s_ref, slope_ref, base_ref, own, beside, chunks):
    half = iota((8, LANES), 0) < 4
    for (i, x), c in itertools.product(enumerate(layers), range(chunks)):
        line = pl.ds((x * chunks + c) * 8, 8)
        for t, tile in enumerate(tall_tiles(half, own[line, :], beside[line, :])):
            slope = slope_ref[pl.ds(flat_row(x, c, chunks) + 8 * t, 8), :]
            base = base_ref[pl.ds(flat_row(i, c, chunks) + 8 * t, 8), :]
            s_ref[pl.ds(tall_row(x, c, chunks) + 8 * t, 8), :] = slope * (base + tile)


def edge_kernel(width_x, recv_ref, base_ref, slope_ref, s_ref, low_ref, high_ref, own, beside):
    layer_rows = own.shape[0] // width_x
    chunks = layer_rows // 8
    scatter(recv_ref, own, beside, (0, width_x - HALO), layer_rows)
    layers = (*range(HALO), *range(width_x - HALO, width_x))
    make_layers(layers, s_ref, slope_ref, base_ref, own, beside, chunks)
    fill_faces(s_ref, low_ref, high_ref, width_x, chunks, tall_row)


def make_edges(recv, base, slope, shape):
    width_x, width_y, width_z = shape
    face = face_shape(shape)
    scratch = pltpu.VMEM((width_x * width_y * width_z // LANES, LANES), F32)
    return pl.pallas_call(
        functools.partial(edge_kernel, width_x),
        out_shape=(extended(shape), face, face),
        in_specs=[VMEM] * 3,
        out_specs=(VMEM,) * 3,
        scratch_shapes=[scratch] * 2,
        compiler_params=params(8),
    )(recv, base, slope)


def weight_of(k):
    return (25.0 / 4.0) ** k / 25.0


def sweep(ref, source, base, k, chunks):
    layer = chunks * TALL
    lane = iota((8, LANES), 1)
    own = [ref[pl.ds(base + c * TALL, 8), :] for c in range(chunks)]
    up = [pltpu.roll(t, LANES - 1, 1) for t in own]
    down = [pltpu.roll(t, 1, 1) for t in own]
    zero = jnp.zeros((8, LANES), F32)
    results = []
    for c in range(chunks):
        at = base + c * TALL
        total = jnp.where(lane == LANES - 1, up[c + 1] if c + 1 < chunks else zero, up[c])
        total = total + jnp.where(lane == 0, down[c - 1] if c else zero, down[c])
        total = total + (ref[pl.ds(at - 1, 8), :] + ref[pl.ds(at + 1, 8), :])
        total = total + (ref[pl.ds(at - layer, 8), :] + ref[pl.ds(at + layer, 8), :])
        results.append(total + weight_of(k) * source[pl.ds(at, 8), :])
    return results


def sweep_layer(old, new, source, x, k, rims, keep, chunks):
    for tile in range(2):
        mask = rims[tile] if keep is None else rims[tile] * keep
        base = tall_row(x, 0, chunks) + 8 * tile
        for c, value in enumerate(sweep(old, source, base, k, chunks)):
            new[pl.ds(base + c * TALL, 8), :] = value * mask


def last_layer(old, source, x, chunks):
    scale = (4.0 / 25.0) ** SWEEPS
    return [scale * t for t in sweep(old, source, tall_row(x, 0, chunks) + HALO, SWEEPS, chunks)]


def store_layer(ref, x, values):
    for c, value in enumerate(values):
        ref[x, :, pl.ds(c * LANES, LANES)] = value


def load_layer(ref, x, chunks):
    return [ref[x, :, pl.ds(c * LANES, LANES)] for c in range(chunks)]


def add_products(total, left, right):
    for a, b in zip(left, right):
        total = total + a * b
    return total


def zero_tile():
    return jnp.zeros((8, LANES), F32)


def inner_sweeps(refs, masks_ref, width_x, chunks):
    rims = (masks_ref[RIM], masks_ref[RIM + 1])
    for k in range(1, SWEEPS):
        for x in range(k, width_x - k):
            sweep_layer(refs[k - 1], refs[k], refs[0], x, k, rims, None, chunks)
    return [last_layer(refs[SWEEPS - 1], refs[0], x, chunks) for x in range(HALO, width_x - HALO)]


def outer_sweeps(refs, masks_ref, width_x, chunks):
    rims = (masks_ref[RIM], masks_ref[RIM + 1])
    for k in range(1, SWEEPS):
        for x in range(k - HALO, k):
            sweep_layer(refs[k - 1], refs[k], refs[0], x, k, rims, masks_ref[LEFT] if x < 0 else None, chunks)
            x = width_x - 1 - x
            keep = masks_ref[RIGHT] if x >= width_x else None
            sweep_layer(refs[k - 1], refs[k], refs[0], x, k, rims, keep, chunks)
    layers = (*range(HALO), *range(width_x - HALO, width_x))
    return [last_layer(refs[SWEEPS - 1], refs[0], x, chunks) for x in layers]


def half_block(shape):
    return jax.ShapeDtypeStruct((shape[0] - 2 * HALO,) + shape[1:], F32), jax.ShapeDtypeStruct(
        (2 * HALO,) + shape[1:], F32
    )


TILE = jax.ShapeDtypeStruct((8, LANES), F32)


def slope_inner_kernel(
    width_x, slope_ref, masks_ref, base_hbm, s_ref, one, two, three, raw_ref, square_ref, base_ref, sems
):
    copies = start_all(((base_hbm, base_ref),), sems)
    chunks = raw_ref.shape[2] // LANES
    s_ref[pl.ds(tall_row(0, 0, chunks), slope_ref.shape[0]), :] = slope_ref[...]
    total = zero_tile()
    for i, values in enumerate(inner_sweeps((s_ref, one, two, three), masks_ref, width_x, chunks)):
        store_layer(raw_ref, i, values)
        total = add_products(total, values, values)
    square_ref[...] = total
    for copy in copies:
        copy.wait()


def make_slope_inner(s, masks, base, shape):
    wide = extended(shape)
    return pl.pallas_call(
        functools.partial(slope_inner_kernel, shape[0]),
        out_shape=(wide, wide, wide, wide, half_block(shape)[0], TILE)
        + (jax.ShapeDtypeStruct(base.shape, F32),),
        in_specs=[VMEM] * 2 + [HBM],
        out_specs=(VMEM,) * 7,
        scratch_shapes=[pltpu.SemaphoreType.DMA((1,))],
        compiler_params=params(8),
        cost_estimate=pl.CostEstimate(flops=15_000_000, bytes_accessed=8_000_000, transcendentals=0),
    )(s, masks, in_hbm(base))


def slope_outer_kernel(
    width_x, left_ref, right_ref, masks_ref, inner_square_ref, s_in, one_in, two_in, three_in,
    s_ref, one, two, three, raw_ref, square_ref,
):
    del s_in, one_in, two_in, three_in
    chunks = raw_ref.shape[2] // LANES
    read_faces(s_ref, left_ref, right_ref, masks_ref, width_x, chunks)
    total = inner_square_ref[...]
    for i, values in enumerate(outer_sweeps((s_ref, one, two, three), masks_ref, width_x, chunks)):
        store_layer(raw_ref, i, values)
        total = add_products(total, values, values)
    square_ref[...] = total


def make_slope_outer(left, right, masks, square, wide, shape):
    same = extended(shape)
    return pl.pallas_call(
        functools.partial(slope_outer_kernel, shape[0]),
        out_shape=(same, same, same, same, half_block(shape)[1], TILE),
        in_specs=[VMEM] * 8,
        out_specs=(VMEM,) * 6,
        input_output_aliases={4: 0, 5: 1, 6: 2, 7: 3},
        compiler_params=params(8),
        cost_estimate=pl.CostEstimate(flops=10_000_000, bytes_accessed=6_000_000, transcendentals=0),
    )(left, right, masks, square, *wide)[4:]


def source_inner_kernel(
    shape, recv_ref, base_ref, slope_ref, masks_ref, slope_raw_ref, edges_ref, s_ref, one, two, three, raw_ref, sums_ref, own, beside,
):
    del edges_ref
    width_x, width_y, width_z = shape
    chunks = width_z // LANES
    scatter(recv_ref, own, beside, range(HALO, width_x - HALO, HALO), width_y * chunks)
    make_layers(range(HALO, width_x - HALO), s_ref, slope_ref, base_ref, own, beside, chunks)
    aa, ab = zero_tile(), zero_tile()
    for i, values in enumerate(inner_sweeps((s_ref, one, two, three), masks_ref, width_x, chunks)):
        store_layer(raw_ref, i, values)
        aa = add_products(aa, values, values)
        ab = add_products(ab, values, load_layer(slope_raw_ref, i, chunks))
    sums_ref[0] = aa
    sums_ref[1] = ab


def make_source_inner(recv, base, slope, masks, slope_raw, edges, shape):
    wide = extended(shape)
    scratch = pltpu.VMEM((shape[0] * shape[1] * shape[2] // LANES, LANES), F32)
    return pl.pallas_call(
        functools.partial(source_inner_kernel, shape),
        out_shape=(wide,) * 4 + (half_block(shape)[0], jax.ShapeDtypeStruct((2, 8, LANES), F32)),
        in_specs=[VMEM] * 6,
        out_specs=(VMEM,) * 6,
        input_output_aliases={5: 0},
        scratch_shapes=[scratch] * 2,
        compiler_params=params(8),
        cost_estimate=pl.CostEstimate(flops=40_000_000, bytes_accessed=16_000_000, transcendentals=0),
    )(recv, base, slope, masks, slope_raw, edges)


def source_outer_kernel(
    width_x, left_ref, right_ref, masks_ref, slope_raw_ref, volume_ref, sums_ref, square_ref,
    s_in, one_in, two_in, three_in,
    s_ref, one, two, three, raw_ref, send_ref,
):
    del s_in, one_in, two_in, three_in
    chunks = raw_ref.shape[2] // LANES
    read_faces(s_ref, left_ref, right_ref, masks_ref, width_x, chunks)
    aa, ab = sums_ref[0], sums_ref[1]
    for i, values in enumerate(outer_sweeps((s_ref, one, two, three), masks_ref, width_x, chunks)):
        store_layer(raw_ref, i, values)
        aa = add_products(aa, values, values)
        ab = add_products(ab, values, load_layer(slope_raw_ref, i, chunks))
    lane = iota((1, LANES), 1)
    line = jnp.zeros((1, LANES), F32)
    for i, tile in enumerate((volume_ref[...], aa, ab, square_ref[...])):
        total = jnp.sum(tile, axis=0, keepdims=True)
        total = total + pltpu.roll(total, LANES // 2, 1)
        total = total + pltpu.roll(total, LANES // 4, 1)
        line = jnp.where(lane // (LANES // 4) == i, total, line)
    send_ref[...] = jnp.broadcast_to(line, send_ref.shape)


def make_source_outer(left, right, masks, slope_raw, volume, sums, square, wide, copies, shape):
    same = jax.ShapeDtypeStruct(wide[0].shape, F32)
    return pl.pallas_call(
        functools.partial(source_outer_kernel, shape[0]),
        out_shape=(same,) * 4 + (half_block(shape)[1], jax.ShapeDtypeStruct((copies, LANES), F32)),
        in_specs=[VMEM] * 11,
        out_specs=(VMEM,) * 6,
        input_output_aliases={7: 0, 8: 1, 9: 2, 10: 3},
        compiler_params=params(8),
    )(left, right, masks, slope_raw, volume, sums, square, *wide)[4:]


def adam_kernel(
    cells, sums_ref, masks_ref, inner_ref, outer_ref, slope_inner_ref, slope_outer_ref, design_ref, first_ref, second_ref,
    d_hbm, m_hbm, v_hbm, g_hbm, d_ref, m_ref, v_ref, g_ref, sems,
):
    width_x = design_ref.shape[0]
    line = jnp.sum(sums_ref[...], axis=0, keepdims=True)
    part = iota(line.shape, 1) // (LANES // 4)

    def picked(scale):
        return jnp.sum(line * scale, axis=1, keepdims=True)

    volume = picked(jnp.where(part == 0, 1.0, 0.0))
    shift = masks_ref[PENALTY, 0:1, 0:1] * (volume / cells / 0.4 - 1.25)
    total = picked(
        jnp.where(part == 1, 1.0, jnp.where(part == 2, 2.0 * shift, jnp.where(part == 3, shift * shift, 0.0)))
    )
    inverse = 1.0 / jnp.sqrt(jnp.maximum(total, 0.0) / cells + 1e-06)
    blocks = width_x // HALO
    copies = []
    for block in range(blocks):
        part = pl.ds(block * HALO, HALO)
        if block in (0, blocks - 1):
            raw, slope_raw, start = outer_ref, slope_outer_ref, 0 if block == 0 else HALO
        else:
            raw, slope_raw, start = inner_ref, slope_inner_ref, (block - 1) * HALO
        for i in range(HALO):
            x = block * HALO + i
            gradient = (raw[start + i] + shift * slope_raw[start + i]) * inverse
            new_first = 0.9 * first_ref[x] + 0.1 * gradient
            new_second = 0.999 * second_ref[x] + 0.001 * gradient * gradient
            first_hat = new_first * (0.05 / (1.0 - 0.9**ADAM_STEP))
            second_hat = new_second * (1.0 / (1.0 - 0.999**ADAM_STEP))
            d_ref[x] = jnp.clip(design_ref[x] - first_hat / (jnp.sqrt(second_hat) + 1e-08), 0.0, 1.0)
            m_ref[x] = new_first
            v_ref[x] = new_second
            g_ref[x] = gradient
        for i, (ref, hbm) in enumerate(((d_ref, d_hbm), (m_ref, m_hbm), (v_ref, v_hbm), (g_ref, g_hbm))):
            copy = pltpu.make_async_copy(ref.at[part], hbm.at[part], sems.at[block, i])
            copy.start()
            copies.append(copy)
    for copy in copies:
        copy.wait()


def adam(cells, sums, masks, parts, design, first_moment, second_moment):
    return pl.pallas_call(
        functools.partial(adam_kernel, cells),
        out_shape=(jax.ShapeDtypeStruct(design.shape, F32),) * 4,
        in_specs=[VMEM] * 9,
        out_specs=(HBM,) * 4,
        scratch_shapes=[pltpu.VMEM(design.shape, F32)] * 4 + [pltpu.SemaphoreType.DMA((4, 4))],
        compiler_params=params(8),
    )(sums, masks, *parts, design, first_moment, second_moment)


def shift(cells, axis, by):
    count = lax.axis_size(axis)
    return lax.ppermute(cells, axis, [(i, (i + by) % count) for i in range(count)])


def per_device(
    design,
    filtered,
    sensitivity,
    first_moment,
    second_moment,
    lagrange,
    trace_values,
    trace_anchor,
    trace_owner,
):
    width_x, width_y, depth = design.shape
    count_x, count_y = lax.axis_size("gx"), lax.axis_size("gy")
    cells = float(width_x * width_y * depth * count_x * count_y)
    rows = trace_values.shape[1]
    low, high, masks, packed, anchors = make_first(
        trace_values[0], trace_anchor, trace_owner.reshape(1, rows), lagrange.reshape(1, 2), filtered, sensitivity, count_y
    )
    below, above = shift(high, "gy", 1), shift(low, "gy", -1)
    sent = make_send(packed, anchors)
    received = lax.all_to_all(sent.reshape(count_y, SENT * LANES), "gy", 0, 0, tiled=True).reshape(sent.shape)

    slope, base_edges, base, low, high, volume = make_slope(filtered, sensitivity, above, below, masks)
    left, right = shift(high, "gx", 1), shift(low, "gx", -1)
    shape = design.shape
    *wide, slope_inner, square, base = make_slope_inner(slope, masks, base, shape)
    slope_outer, square = make_slope_outer(left, right, masks, square, wide, shape)

    source, low, high = make_edges(received, base_edges, slope, shape)
    left, right = shift(high, "gx", 1), shift(low, "gx", -1)
    *wide, inner, sums = make_source_inner(received, base, slope, masks, slope_inner, source, shape)
    outer, sums = make_source_outer(
        left, right, masks, slope_outer, volume, sums, square, wide, count_x * count_y, shape
    )
    sums = lax.all_to_all(sums, ("gx", "gy"), 0, 0, tiled=True)
    parts = (inner, outer, slope_inner, slope_outer)
    return adam(cells, sums, masks, parts, design, first_moment, second_moment)


def solution(mesh):
    block = P("gx", "gy", None)
    return jax.shard_map(
        per_device,
        mesh=mesh,
        in_specs=(block, block, block, block, block, P(), block, P("gx", "gy"), block),
        out_specs=(block, block, block, block),
        check_vma=False,
    )
```
